128 devices in a mesh: tm: 4 (over y), space: 32 (over z, x, core).
Axes of the slice: x: 4, y: 4, z: 4, core: 2. Of those that a mesh axis runs over, the one named last changes fastest.
Arguments:
- spectra: bfloat16 [2, 8, 4, 64, 4, 4096], P(None, 'tm', None, None, None, 'space'), may hold values from -6 to 6
- weights: float32 [4, 4096], P(None, 'space'), may hold values from 0.25 to 4
Outputs:
- modes: bfloat16 [2, 8, 4, 64, 4, 4096], P(None, None, 'tm', None, None, 'space')
- upper: float32 [2, 8, 4, 64, 64], P(None, None, 'tm')
The draws below stay inside these ranges and needn't reach their ends.
All inputs are finite; a program needn't handle non-finite values.
Results may differ from the reference program's by a relative error of at most 0.009.
Values may be sent and summed in bfloat16 or wider, within the bound.
No kernel may reach another device: no remote copies, remote signals or barrier semaphores. Data moves between devices by JAX's collectives and lax.ppermute only.
A program may use at most 128 MiB of HBM per device.

```python
import math
import jax
import jax.numpy as jnp
from jax import lax

NSUB = 8
C = 64
FIELDS = 4
M = 4
PTS = 4096


def block_levels(stream_key, extent, cuts, smallest, high):
    def one(position, parts):
        steps = jax.random.uniform(jax.random.fold_in(jax.random.fold_in(stream_key, 6), position), (parts,), jnp.float32, smallest / len(cuts), high / len(cuts))
        return jnp.repeat(jnp.exp(steps), extent[position] // parts).reshape((-1,) + (1,) * (len(extent) - position - 1))

    level = one(*cuts[0])
    for cut in cuts[1:]:
        level = level * one(*cut)
    return level


def centred(own_key, extent, spread, most, cuts=(), held_as=jnp.bfloat16):
    loudness = block_levels(own_key, extent, cuts, -0.22, 0.18) if cuts else 1.0
    entries = jax.random.normal(own_key, extent, jnp.float32) * spread * loudness
    return jnp.minimum(jnp.maximum(entries, -most), most).astype(held_as)


def setup_inputs(seed: int = 0) -> dict:
    key_list = jax.random.split(jax.random.key(seed), 3)
    spectra = centred(key_list[0], (2, NSUB, M, C, FIELDS, PTS), 1.0, 6.0, ((1, 4), (5, 32)))
    weights = jnp.clip(jnp.exp(math.log(4.0) - 2.7725887 * jax.random.uniform(key_list[1], (FIELDS, PTS), jnp.float32) ** block_levels(key_list[1], (FIELDS, PTS), ((1, 32),), -0.2, 0.2)), 0.25, 4.0)
    return {"spectra": spectra, "weights": weights}


HIGHEST = lax.Precision.HIGHEST
TWO_PI = 2.0 * math.pi

def cholesky_upper(gram_real, gram_imag):
    width = gram_real.shape[0]
    counter = jnp.arange(width, dtype=jnp.int32)

    def advance(column, carry):
        work_real, work_imag, upper_real, upper_imag = carry
        row_real = lax.dynamic_index_in_dim(work_real, column, 0, keepdims=False)
        row_imag = lax.dynamic_index_in_dim(work_imag, column, 0, keepdims=False)
        on_diag = (counter == column)[:, None]
        pivot = jnp.sqrt(lax.optimization_barrier(jnp.sum(jnp.where(on_diag, row_real, 0.0), axis=0)))
        row_real = jnp.where((counter >= column)[:, None], row_real, 0.0) / pivot
        row_imag = jnp.where((counter > column)[:, None], row_imag, 0.0) / pivot
        work_real = work_real - (row_real[:, None] * row_real[None] + row_imag[:, None] * row_imag[None])
        work_imag = work_imag - (row_real[:, None] * row_imag[None] - row_imag[:, None] * row_real[None])
        upper_real = lax.dynamic_update_index_in_dim(upper_real, row_real, column, 0)
        upper_imag = lax.dynamic_update_index_in_dim(upper_imag, row_imag, column, 0)
        return (work_real, work_imag, upper_real, upper_imag)
    zeros = jnp.zeros_like(gram_real)
    result = lax.fori_loop(0, width, advance, (gram_real, gram_imag, zeros, zeros))
    return (result[2], result[3])

def upper_inverse(upper_real, upper_imag):
    width = upper_real.shape[0]
    counter = jnp.arange(width, dtype=jnp.int32)

    def advance(offset, carry):
        inverse_real, inverse_imag = carry
        column = width - 1 - offset
        row_real = lax.dynamic_index_in_dim(upper_real, column, 0, keepdims=False)
        row_imag = lax.dynamic_index_in_dim(upper_imag, column, 0, keepdims=False)
        on_diag = (counter == column)[:, None]
        pivot = lax.optimization_barrier(jnp.sum(jnp.where(on_diag, row_real, 0.0), axis=0))
        sum_real = lax.optimization_barrier(jnp.sum(row_real[:, None] * inverse_real - row_imag[:, None] * inverse_imag, axis=0))
        sum_imag = lax.optimization_barrier(jnp.sum(row_real[:, None] * inverse_imag + row_imag[:, None] * inverse_real, axis=0))
        unit = jnp.where(on_diag, 1.0, 0.0).astype(upper_real.dtype)
        new_real = (unit - sum_real) / pivot
        new_imag = -sum_imag / pivot
        inverse_real = lax.dynamic_update_index_in_dim(inverse_real, new_real, column, 0)
        inverse_imag = lax.dynamic_update_index_in_dim(inverse_imag, new_imag, column, 0)
        return (inverse_real, inverse_imag)
    zeros = jnp.zeros_like(upper_real)
    return lax.fori_loop(0, width, advance, (zeros, zeros))

def data_gram(data_real, data_imag, row_weight):
    weighted_real = data_real * row_weight
    weighted_imag = data_imag * row_weight
    gram_real = jnp.einsum('bcs,bds->cdb', weighted_real, data_real, precision=HIGHEST) + jnp.einsum('bcs,bds->cdb', weighted_imag, data_imag, precision=HIGHEST)
    gram_imag = jnp.einsum('bcs,bds->cdb', weighted_real, data_imag, precision=HIGHEST) - jnp.einsum('bcs,bds->cdb', weighted_imag, data_real, precision=HIGHEST)
    return (gram_real, gram_imag)

def apply_inverse(data_real, data_imag, inverse_real, inverse_imag):
    mode_real = jnp.einsum('bcs,clb->bls', data_real, inverse_real, precision=HIGHEST) - jnp.einsum('bcs,clb->bls', data_imag, inverse_imag, precision=HIGHEST)
    mode_imag = jnp.einsum('bcs,clb->bls', data_real, inverse_imag, precision=HIGHEST) + jnp.einsum('bcs,clb->bls', data_imag, inverse_real, precision=HIGHEST)
    return jnp.stack([mode_real, mode_imag]).astype(jnp.bfloat16)

def reference(spectra, weights):
    sub_count = spectra.shape[1]
    freq_total = sub_count * M
    row_weight = weights.reshape(-1)
    sub_index = jnp.arange(sub_count, dtype=jnp.int32)

    def per_bin(bin_index):
        block = lax.dynamic_index_in_dim(spectra, bin_index, 2, keepdims=False).astype(jnp.float32)
        block = block.reshape(2, sub_count, C, -1)
        phase = sub_index[None, :] * (bin_index + M * sub_index[:, None]) % freq_total
        angle = -TWO_PI / freq_total * phase.astype(jnp.float32)
        kernel_real = jnp.cos(angle)
        kernel_imag = jnp.sin(angle)
        data_real = jnp.einsum('qr,rcs->qcs', kernel_real, block[0], precision=HIGHEST) - jnp.einsum('qr,rcs->qcs', kernel_imag, block[1], precision=HIGHEST)
        data_imag = jnp.einsum('qr,rcs->qcs', kernel_real, block[1], precision=HIGHEST) + jnp.einsum('qr,rcs->qcs', kernel_imag, block[0], precision=HIGHEST)
        gram_real, gram_imag = data_gram(data_real, data_imag, row_weight)
        upper_real, upper_imag = cholesky_upper(gram_real, gram_imag)
        inverse_real, inverse_imag = upper_inverse(upper_real, upper_imag)
        bin_modes = apply_inverse(data_real, data_imag, inverse_real, inverse_imag)
        bin_upper = jnp.stack([jnp.transpose(upper_real, (2, 0, 1)), jnp.transpose(upper_imag, (2, 0, 1))])
        return (bin_modes, bin_upper)
    all_modes, all_upper = lax.map(per_bin, jnp.arange(M, dtype=jnp.int32))
    all_modes = jnp.moveaxis(all_modes, 0, 2).reshape(2, sub_count, M, C, FIELDS, -1)
    all_upper = jnp.moveaxis(all_upper, 0, 2)
    return (all_modes, all_upper)
```

```python
import math

import jax
import jax.numpy as jnp
import numpy as np
from jax import lax
from jax.experimental import pallas as pl
from jax.experimental.pallas import tpu as pltpu
from jax.sharding import PartitionSpec as P

SUBS = 8
WIDTH = 64
FIELDS = 4
LANES = 128
ROWS = WIDTH * FIELDS
F32 = jnp.float32
BF16 = jnp.bfloat16


def twiddle_table():
    table = np.zeros((4, 16), np.float32)
    for t in range(4):
        for d in range(4):
            angle = -2.0 * math.pi * (((t - d) % 4) * t) / 16.0
            table[t, 2 * d] = math.cos(angle)
            table[t, 2 * d + 1] = math.sin(angle)
        for q in range(4):
            angle = -2.0 * math.pi * (t / 32.0 + q / 8.0)
            table[t, 8 + 2 * q] = math.cos(angle)
            table[t, 9 + 2 * q] = math.sin(angle)
    return table


def phase_table():
    table = np.zeros((4, 16), np.float32)
    for t in range(4):
        for q in range(8):
            re, im = [(1, 0), (0, -1), (-1, 0), (0, 1)][(t * q) % 4]
            table[t, 2 * q] = re
            table[t, 2 * q + 1] = im
    return table


def split(value):
    high = value.astype(BF16)
    return high, (value - high.astype(F32)).astype(BF16)


def lane_iota(shape):
    return lax.broadcasted_iota(jnp.int32, shape, len(shape) - 1)


def gram_kernel(own, near1, near2, near3, weight16, twiddle, sh_ref, sl_ref, gram_ref, work):
    t = lax.axis_index("tm")
    root = jnp.sqrt(weight16[...])
    sources = (own, near1, near2, near3)
    tw = [(root * twiddle[t, 2 * d], root * twiddle[t, 2 * d + 1]) for d in range(4)]
    tq = [(twiddle[t, 8 + 2 * q], twiddle[t, 9 + 2 * q]) for q in range(4)]

    def transform(step, _):
        row = pl.multiple_of(step * 16, 16)
        rows = pl.ds(row, 16)
        radix = []
        for s in range(2):
            y = []
            for d in range(4):
                re = sources[d][0, s, rows, :].astype(F32)
                im = sources[d][1, s, rows, :].astype(F32)
                y.append((re * tw[d][0] - im * tw[d][1], re * tw[d][1] + im * tw[d][0]))
            a = (y[0][0] + y[2][0], y[0][1] + y[2][1])
            b = (y[0][0] - y[2][0], y[0][1] - y[2][1])
            c = (y[1][0] + y[3][0], y[1][1] + y[3][1])
            e = (y[1][0] - y[3][0], y[1][1] - y[3][1])
            radix.append(
                [
                    (a[0] + c[0], a[1] + c[1]),
                    (b[0] - e[1], b[1] + e[0]),
                    (a[0] - c[0], a[1] - c[1]),
                    (b[0] + e[1], b[1] - e[0]),
                ]
            )
        for q in range(4):
            x0 = radix[0][q]
            x1 = radix[1][q]
            v = (x1[0] * tq[q][0] - x1[1] * tq[q][1], x1[0] * tq[q][1] + x1[1] * tq[q][0])
            work[q, 0, rows, :] = x0[0] + v[0]
            work[q, 1, rows, :] = x0[1] + v[1]
            work[q + 4, 0, rows, :] = x0[0] - v[0]
            work[q + 4, 1, rows, :] = x0[1] - v[1]
        return 0

    lax.fori_loop(0, ROWS // 16, transform, 0)

    lane = lane_iota((WIDTH, LANES))
    line = lax.broadcasted_iota(jnp.int32, (WIDTH, LANES), 0)
    left = lane < WIDTH
    keep = (lane % WIDTH) >= line

    def one_gram(q):
        for part in range(2):
            for f in range(FIELDS):
                value = work[q, part, pl.ds(f, WIDTH, stride=FIELDS), :]
                high, low = split(value)
                sh_ref[q, part * WIDTH : (part + 1) * WIDTH, f * LANES : (f + 1) * LANES] = high
                sl_ref[q, part * WIDTH : (part + 1) * WIDTH, f * LANES : (f + 1) * LANES] = low
        high = sh_ref[q]
        both = jnp.concatenate([high, sl_ref[q]], axis=0)
        prod = lax.dot_general(both, high, (((1,), (1,)), ((), ())), preferred_element_type=F32)
        cross = prod[LANES:]
        full = prod[:LANES] + (cross + cross.T)
        low = pltpu.roll(full[WIDTH:], WIDTH, 1)
        return full[:WIDTH] + jnp.where(left, low, -low)

    def pair(index, _):
        first = one_gram(2 * index)
        second = one_gram(2 * index + 1)
        first_r = pltpu.roll(first, WIDTH, 1)
        second_r = pltpu.roll(second, WIDTH, 1)
        gram_ref[pl.ds(pl.multiple_of(index * WIDTH, WIDTH), WIDTH), :] = jnp.where(
            left, jnp.where(keep, first, first_r), jnp.where(keep, second_r, second)
        )
        return 0

    lax.fori_loop(0, SUBS // 2, pair, 0)


def lane_at(value, lane):
    return jnp.broadcast_to(value[:, lane : lane + 1], value.shape)


def factor_kernel(gram, sh_ref, sl_ref, weight, phase, modes_ref, upper_ref, work, spread):
    t = lax.axis_index("tm")
    wide = (WIDTH, LANES)
    lane = lane_iota(wide)
    column = lane % WIDTH
    line = lax.broadcasted_iota(jnp.int32, wide, 0)
    left = lane < WIDTH
    for pair in range(SUBS // 2):
        packed = gram[pair * WIDTH : (pair + 1) * WIDTH, :]
        turned = jnp.concatenate([packed, packed], axis=0).T
        work[pl.ds(2 * pair * WIDTH, WIDTH), :] = jnp.where(left, packed, -turned[:WIDTH])
        rolled = pltpu.roll(packed, WIDTH, 1)
        work[pl.ds((2 * pair + 1) * WIDTH, WIDTH), :] = jnp.where(left, rolled, -turned[WIDTH:])
    rows = [work[pl.ds(i, SUBS, stride=WIDTH), :] for i in range(WIDTH)]

    small = (SUBS, LANES)
    lane8 = lane_iota(small)
    sign = jnp.where(lane8 < WIDTH, 1.0, -1.0).astype(F32)
    zero = jnp.zeros(small, F32)

    def turn(value):
        return pltpu.roll(value, WIDTH, 1) * sign

    for k in range(WIDTH // 2):
        c0 = 2 * k
        c1 = c0 + 1
        a, b = rows[c0], rows[c1]
        at0 = (lane8 == c0) | (lane8 == WIDTH + c0)
        at1 = (lane8 == c1) | (lane8 == WIDTH + c1)
        p1 = lane_at(a, c0)
        ar = lane_at(a, c1)
        ai = lane_at(a, WIDTH + c1)
        p2 = lane_at(b, c1)
        one0 = jnp.where(lane8 == c0, 1.0, 0.0).astype(F32)
        one1 = jnp.where(lane8 == c1, 1.0, 0.0).astype(F32)
        ae = jnp.where(at0, one0, a)
        ae_t = turn(ae)
        b0 = jnp.where(at0, 0.0, b)
        b0_t = turn(b0)
        i1 = 1.0 / p1
        mr = ar * i1
        mi = ai * i1
        d = p2 - (ar * mr + ai * mi)
        i2 = 1.0 / d
        bn = b0 - mr * ae - mi * ae_t
        bn_t = b0_t - mr * ae_t + mi * ae
        be = jnp.where(at1, one1, bn)
        one1_t = jnp.where(lane8 == WIDTH + c1, -1.0, 0.0).astype(F32)
        be_t = jnp.where(at1, one1_t, bn_t)
        y1 = jnp.where(at1, 0.0, ae) * i1
        y1_t = jnp.where(at1, 0.0, ae_t) * i1
        y2 = be * i2
        y2_t = be_t * i2
        clear = at0 | at1
        for i in range(c0 + 2, WIDTH):
            rows[i] = (
                jnp.where(clear, 0.0, rows[i])
                - (lane_at(a, i) * y1 + lane_at(a, WIDTH + i) * y1_t)
                - (lane_at(bn, i) * y2 + lane_at(bn, WIDTH + i) * y2_t)
            )
        spread[c0 * SUBS : (c0 + 1) * SUBS, :] = ae * lax.rsqrt(p1)
        spread[c1 * SUBS : (c1 + 1) * SUBS, :] = be * lax.rsqrt(d)

    root = lax.rsqrt(weight[...])

    def emit(q, _):
        both = spread[pl.ds(q, WIDTH, stride=SUBS), :]
        inverse = jnp.where(column <= line, both, 0.0)
        diag = jnp.where(left, 1.0 / both, 0.0)
        upper = jnp.where(column > line, both, jnp.where(column == line, diag, 0.0))
        upper_ref[0, q] = upper[:, :WIDTH]
        upper_ref[1, q] = upper[:, WIDTH:]
        swapped = pltpu.roll(inverse, WIDTH, 1)
        swapped = jnp.where(left, -swapped, swapped)
        pr = phase[t, 2 * q]
        pi = phase[t, 2 * q + 1]
        lhs = jnp.concatenate([pr * inverse - pi * swapped, pr * swapped + pi * inverse], axis=0)
        lh, ll = split(lhs)
        sh = sh_ref[q]
        out = jnp.dot(lh, sh, preferred_element_type=F32)
        out = out + jnp.dot(ll, sh, preferred_element_type=F32)
        out = out + jnp.dot(lh, sl_ref[q], preferred_element_type=F32)
        for part in range(2):
            for f in range(FIELDS):
                block = out[part * WIDTH : (part + 1) * WIDTH, f * LANES : (f + 1) * LANES]
                work[pl.ds(part * ROWS + f, WIDTH, stride=FIELDS), :] = block * root[f : f + 1, :]
            modes_ref[part, q] = work[part * ROWS : (part + 1) * ROWS, :].astype(BF16)
        return 0

    lax.fori_loop(0, SUBS, emit, 0)


def vmem():
    return pl.BlockSpec(memory_space=pltpu.VMEM)


def smem():
    return pl.BlockSpec(memory_space=pltpu.SMEM)


def run_gram(own, near, weight16, table):
    return pl.pallas_call(
        gram_kernel,
        name="gram",
        out_shape=(
            jax.ShapeDtypeStruct((SUBS, LANES, FIELDS * LANES), BF16),
            jax.ShapeDtypeStruct((SUBS, LANES, FIELDS * LANES), BF16),
            jax.ShapeDtypeStruct((SUBS // 2 * WIDTH, LANES), F32),
        ),
        in_specs=[vmem()] * 5 + [smem()],
        out_specs=(vmem(), vmem(), vmem()),
        scratch_shapes=[pltpu.VMEM((SUBS, 2, ROWS, LANES), F32)],
        compiler_params=pltpu.CompilerParams(vmem_limit_bytes=32 * 1024 * 1024),
    )(own, *near, weight16, table)


def run_factor(gram, sh, sl, weights, table):
    return pl.pallas_call(
        factor_kernel,
        name="factor",
        out_shape=(
            jax.ShapeDtypeStruct((2, SUBS, ROWS, LANES), BF16),
            jax.ShapeDtypeStruct((2, SUBS, WIDTH, WIDTH), F32),
        ),
        in_specs=[vmem()] * 4 + [smem()],
        out_specs=(vmem(), vmem()),
        scratch_shapes=[
            pltpu.VMEM((SUBS * WIDTH, LANES), F32),
            pltpu.VMEM((SUBS * WIDTH, LANES), F32),
        ],
        compiler_params=pltpu.CompilerParams(vmem_limit_bytes=32 * 1024 * 1024),
    )(gram, sh, sl, weights, table)


def space_perm(along, shift):
    pairs = []
    for i in range(32):
        z, x, core = i // 8, i // 2 % 4, i % 2
        if along == "x":
            x = (x + shift) % 4
        elif along == "z":
            z = (z + shift) % 4
        else:
            core = 1 - core
        pairs.append((i, (z * 4 + x) * 2 + core))
    return pairs


def sum_over_space(value):
    value = value + lax.ppermute(value, "space", space_perm("core", 1))
    for along in ("x", "z"):
        far = [lax.ppermute(value, "space", space_perm(along, d)) for d in (1, 3, 2)]
        value = (value + far[2]) + (far[0] + far[1])
    return value


def on_device(spectra, weights):
    t = lax.axis_index("tm")
    flat = spectra.reshape(2, 2, 4, ROWS, LANES)
    own = lax.dynamic_index_in_dim(flat, t, 2, keepdims=False)
    near = []
    for d in range(1, 4):
        piece = lax.dynamic_index_in_dim(flat, (t + d) % 4, 2, keepdims=False)
        near.append(lax.ppermute(piece, "tm", [(i, (i + d) % 4) for i in range(4)]))
    weight16 = jnp.tile(weights, (4, 1))
    sh, sl, gram = run_gram(own, near, weight16, jnp.asarray(twiddle_table()))
    gram = sum_over_space(gram)
    modes, upper = run_factor(gram, sh, sl, weights, jnp.asarray(phase_table()))
    return (
        modes.reshape(2, SUBS, 1, WIDTH, FIELDS, LANES),
        upper.reshape(2, SUBS, 1, WIDTH, WIDTH),
    )


def solution(mesh):
    placed = (P(None, "tm", None, None, None, "space"), P(None, "space"))
    return jax.shard_map(
        on_device,
        mesh=mesh,
        in_specs=placed,
        out_specs=(P(None, None, "tm", None, None, "space"), P(None, None, "tm", None, None)),
        check_vma=False,
    )
```

```python
import math

import jax
import jax.numpy as jnp
import numpy as np
from jax import lax
from jax.experimental import pallas as pl
from jax.experimental.pallas import tpu as pltpu
from jax.sharding import PartitionSpec as P

SUBS = 8
WIDTH = 64
FIELDS = 4
LANES = 128
ROWS = WIDTH * FIELDS
F32 = jnp.float32
BF16 = jnp.bfloat16


def twiddle_table():
    table = np.zeros((4, 16), np.float32)
    for t in range(4):
        for d in range(4):
            angle = -2.0 * math.pi * (((t - d) % 4) * t) / 16.0
            table[t, 2 * d] = math.cos(angle)
            table[t, 2 * d + 1] = math.sin(angle)
        for q in range(4):
            angle = -2.0 * math.pi * (t / 32.0 + q / 8.0)
            table[t, 8 + 2 * q] = math.cos(angle)
            table[t, 9 + 2 * q] = math.sin(angle)
    return table


def phase_table():
    table = np.zeros((4, 16), np.float32)
    for t in range(4):
        for q in range(8):
            re, im = [(1, 0), (0, -1), (-1, 0), (0, 1)][(t * q) % 4]
            table[t, 2 * q] = re
            table[t, 2 * q + 1] = im
    return table


def split(value):
    high = value.astype(BF16)
    return high, (value - high.astype(F32)).astype(BF16)


def lane_iota(shape):
    return lax.broadcasted_iota(jnp.int32, shape, len(shape) - 1)


SMALL = (8, LANES)


def places():
    lane = lane_iota(SMALL)
    sub = lax.broadcasted_iota(jnp.int32, SMALL, 0)
    parity = lane // WIDTH
    group = lane % 16
    return lane, sub, parity, group, group * 4 + sub % 4


def block_transpose(tiles):
    block = lane_iota(tiles[0].shape) // 16
    for bit in range(3):
        step = 1 << bit
        low = (block & step) == 0
        out = list(tiles)
        for x in range(8):
            if x & step == 0:
                y = x | step
                out[x] = jnp.where(low, tiles[x], pltpu.roll(tiles[y], 16 * step, 1))
                out[y] = jnp.where(low, pltpu.roll(tiles[x], LANES - 16 * step, 1), tiles[y])
        tiles = out
    return tiles


def gather_lanes(value, index):
    return jnp.take_along_axis(value, index, axis=1)


def reverse_rows(value, lane, sub):
    index = (1 - lane // WIDTH) * WIDTH + (lane % WIDTH) // 16 * 16 + 15 - lane % 16
    value = gather_lanes(value, index)
    value = jnp.where(sub % 2 == 0, pltpu.roll(value, 7, 0), pltpu.roll(value, 1, 0))
    return jnp.where(sub % 4 < 2, pltpu.roll(value, 6, 0), pltpu.roll(value, 2, 0))


def gram_kernel(own, near1, near2, near3, weight16, twiddle, sh_ref, sl_ref, keep_ref, send_ref, work, mixed):
    t = lax.axis_index("tm")
    root = jnp.sqrt(weight16[...])
    sources = (own, near1, near2, near3)
    tw = [(root * twiddle[t, 2 * d], root * twiddle[t, 2 * d + 1]) for d in range(4)]
    tq = [(twiddle[t, 8 + 2 * q], twiddle[t, 9 + 2 * q]) for q in range(4)]

    def transform(step, _):
        row = pl.multiple_of(step * 16, 16)
        rows = pl.ds(row, 16)
        radix = []
        for s in range(2):
            y = []
            for d in range(4):
                re = sources[d][0, s, rows, :].astype(F32)
                im = sources[d][1, s, rows, :].astype(F32)
                y.append((re * tw[d][0] - im * tw[d][1], re * tw[d][1] + im * tw[d][0]))
            a = (y[0][0] + y[2][0], y[0][1] + y[2][1])
            b = (y[0][0] - y[2][0], y[0][1] - y[2][1])
            c = (y[1][0] + y[3][0], y[1][1] + y[3][1])
            e = (y[1][0] - y[3][0], y[1][1] - y[3][1])
            radix.append(
                [
                    (a[0] + c[0], a[1] + c[1]),
                    (b[0] - e[1], b[1] + e[0]),
                    (a[0] - c[0], a[1] - c[1]),
                    (b[0] + e[1], b[1] - e[0]),
                ]
            )
        for q in range(4):
            x0 = radix[0][q]
            x1 = radix[1][q]
            v = (x1[0] * tq[q][0] - x1[1] * tq[q][1], x1[0] * tq[q][1] + x1[1] * tq[q][0])
            work[q, 0, rows, :] = x0[0] + v[0]
            work[q, 1, rows, :] = x0[1] + v[1]
            work[q + 4, 0, rows, :] = x0[0] - v[0]
            work[q + 4, 1, rows, :] = x0[1] - v[1]
        return 0

    lax.fori_loop(0, ROWS // 16, transform, 0)

    left = lane_iota((WIDTH, LANES)) < WIDTH

    def one_gram(q):
        for part in range(2):
            for f in range(FIELDS):
                for s in range(4):
                    value = work[q, part, pl.ds(s * 4 + f, 16, stride=16), :]
                    high, low = split(value)
                    place = slice(part * WIDTH + s * 16, part * WIDTH + s * 16 + 16)
                    sh_ref[q, place, f * LANES : (f + 1) * LANES] = high
                    sl_ref[q, place, f * LANES : (f + 1) * LANES] = low
        high = sh_ref[q]
        both = jnp.concatenate([high, sl_ref[q]], axis=0)
        prod = lax.dot_general(both, high, (((1,), (1,)), ((), ())), preferred_element_type=F32)
        cross = prod[LANES:]
        full = prod[:LANES] + (cross + cross.T)
        low = pltpu.roll(full[WIDTH:], WIDTH, 1)
        return full[:WIDTH] + jnp.where(left, low, -low)

    lane, sub, parity, _, column = places()

    def half(base):
        tiles = [None] * 8
        for qq in range(4):
            tile = one_gram(base + qq)
            for p in range(2):
                tiles[p * 4 + qq] = jnp.concatenate(
                    [tile[p * 16 : p * 16 + 16], tile[32 + p * 16 : 48 + p * 16]], axis=0
                )
        for a, tile in enumerate(block_transpose(tiles)):
            mixed[a * 32 : (a + 1) * 32, :] = tile
        out = []
        for m in range(16):
            near = mixed[pl.ds(m % 2 * 16 + m // 2, 8, stride=32), :]
            far_m = 31 - m
            far = mixed[pl.ds(far_m % 2 * 16 + far_m // 2, 8, stride=32), :]
            far = reverse_rows(far, lane, sub)
            line = 2 * m + parity
            far = jnp.where(column == line, pltpu.roll(far, 4, 0), far)
            upper = (column > line) | ((column == line) & (sub < 4))
            out.append(jnp.where(upper, near, far))
        return out

    mine = lax.axis_index("space") % 2
    first = half(0)
    second = half(4)
    for m in range(16):
        keep_ref[m * 8 : (m + 1) * 8, :] = jnp.where(mine == 0, first[m], second[m])
        send_ref[m * 8 : (m + 1) * 8, :] = jnp.where(mine == 0, second[m], first[m])


def at_sub(value, index):
    return jnp.broadcast_to(value[index : index + 1, :], value.shape)


def factor_kernel(gram, out_ref):
    lane, sub, parity, group, column = places()
    first = parity == 0
    sign = jnp.where(sub < 4, 1.0, -1.0).astype(F32)
    real = sub < 4
    lane_base = lane // 16 * 16

    def turn(value):
        return pltpu.roll(value, 4, 0) * sign

    def lifted(value):
        return jnp.where(first, value, pltpu.roll(value, 7, 0))

    rows = [None] * 32
    for m in range(16):
        packed = gram[m * 8 : (m + 1) * 8, :]
        rows[m] = packed
        far = reverse_rows(packed, lane, sub)
        line = 2 * (31 - m) + parity
        rows[31 - m] = jnp.where(column == line, pltpu.roll(far, 4, 0), far)

    for g in range(16):
        pair = (rows[2 * g], rows[2 * g + 1])
        full, block, ahead = [], [], []
        for v in pair:
            turned = pltpu.roll(v, WIDTH, 1)
            one = jnp.where(first, v, turned)
            two = jnp.where(first, turned, v)
            full += [one, two]
            for p in range(2):
                block.append(gather_lanes(v, lane % WIDTH // 16 * 16 + p * WIDTH + g))
        if g < 15:
            for r in range(4):
                ahead.append(gather_lanes(lifted(full[r]), lane_base + g + 1))
        in_group = group == g
        inverse, root, scaled = [], [], []
        for s in range(4):
            here = in_group & (sub % 4 == s)
            pivot = at_sub(block[s], s)
            ip = 1.0 / pivot
            inverse.append(ip)
            root.append(lax.rsqrt(pivot))
            full[s] = jnp.where(here, jnp.where(real, 1.0, 0.0), full[s])
            y = full[s] * ip
            y_t = turn(y)
            b = block[s] * ip
            b_t = turn(b)
            if g < 15:
                n = ahead[s] * ip
                n_t = turn(n)
            for r in range(s + 1, 4):
                mr = at_sub(block[s], r)
                mi = at_sub(block[s], 4 + r)
                full[r] = jnp.where(here, 0.0, full[r]) - mr * y - mi * y_t
                block[r] = block[r] - mr * b - mi * b_t
                if g < 15:
                    ahead[r] = ahead[r] - mr * n - mi * n_t
            later = in_group & (sub % 4 > s)
            y = jnp.where(later, 0.0, y)
            scaled.append((y, jnp.where(later, 0.0, y_t)))
        raised = [lifted(full[r]) for r in range(4)]
        for h in range(g + 1, 16):
            if h == g + 1:
                multi = ahead
            else:
                multi = [gather_lanes(raised[r], lane_base + h) for r in range(4)]
            for odd in range(2):
                m = 2 * h + odd
                value = jnp.where(in_group, 0.0, rows[m])
                terms = []
                for r in range(4):
                    y, y_t = scaled[r]
                    terms.append(at_sub(multi[r], 2 * odd) * y + at_sub(multi[r], 4 + 2 * odd) * y_t)
                rows[m] = value - ((terms[0] + terms[1]) + (terms[2] + terms[3]))
        for odd in range(2):
            m = 2 * g + odd
            out_ref[m * 8 : (m + 1) * 8, :] = jnp.where(
                first, full[2 * odd] * root[2 * odd], full[2 * odd + 1] * root[2 * odd + 1]
            )


def modes_kernel(own, far, sh_ref, sl_ref, weight, phase, modes_ref, upper_ref, turned, work, natural):
    t = lax.axis_index("tm")
    mine = lax.axis_index("space") % 2
    wide = (WIDTH, LANES)
    lane = lane_iota(wide)
    order = lax.broadcasted_iota(jnp.int32, wide, 0)
    line = order % 16 * 4 + order // 16 % 2 * 2 + order // 32
    column = lane % 16 * 4 + lane // 16 % 4
    left = lane < WIDTH
    lane8 = lane_iota(SMALL)
    natural_index = lane8 // WIDTH * WIDTH + lane8 % 4 * 16 + lane8 % WIDTH // 4
    root = lax.rsqrt(weight[...])

    for slot, source in enumerate((own, far)):
        tiles = []
        for a in range(8):
            tiles.append(
                jnp.concatenate(
                    [source[pl.ds(a + 8 * odd, 16, stride=16), :] for odd in range(2)], axis=0
                )
            )
        for b, tile in enumerate(block_transpose(tiles)):
            turned[slot, b % 4, b // 4 * 32 : b // 4 * 32 + 32, :] = tile

    def emit(index, _):
        slot = index // 4
        q = ((mine + slot) % 2) * 4 + index % 4
        both = turned[slot, index % 4]
        inverse = jnp.where(column <= line, both, 0.0)
        diag = jnp.where(left, 1.0 / both, 0.0)
        upper = jnp.where(column > line, both, jnp.where(column == line, diag, 0.0))
        for j in range(4):
            s = 2 * (j % 2) + j // 2
            for k in range(2):
                piece = gather_lanes(upper[j * 16 + k * 8 : j * 16 + k * 8 + 8], natural_index)
                natural[pl.ds(s + 32 * k, 8, stride=4), :] = piece
        upper_ref[0, q] = natural[:, :WIDTH]
        upper_ref[1, q] = natural[:, WIDTH:]
        swapped = pltpu.roll(inverse, WIDTH, 1)
        swapped = jnp.where(left, -swapped, swapped)
        pr = phase[t, 2 * q]
        pi = phase[t, 2 * q + 1]
        lhs = jnp.concatenate([pr * inverse - pi * swapped, pr * swapped + pi * inverse], axis=0)
        lh, ll = split(lhs)
        sh = sh_ref[q]
        out = jnp.dot(lh, sh, preferred_element_type=F32)
        out = out + jnp.dot(ll, sh, preferred_element_type=F32)
        out = out + jnp.dot(lh, sl_ref[q], preferred_element_type=F32)
        for part in range(2):
            for f in range(FIELDS):
                block = out[part * WIDTH : (part + 1) * WIDTH, f * LANES : (f + 1) * LANES] * root[f : f + 1, :]
                for j in range(4):
                    s = 2 * (j % 2) + j // 2
                    work[pl.ds(part * ROWS + s * 4 + f, 16, stride=16), :] = block[j * 16 : j * 16 + 16]
            modes_ref[part, q] = work[part * ROWS : (part + 1) * ROWS, :].astype(BF16)
        return 0

    lax.fori_loop(0, SUBS, emit, 0)


def vmem():
    return pl.BlockSpec(memory_space=pltpu.VMEM)


def smem():
    return pl.BlockSpec(memory_space=pltpu.SMEM)


HALF = (LANES, LANES)
PARAMS = pltpu.CompilerParams(vmem_limit_bytes=32 * 1024 * 1024)


def run_gram(own, near, weight16, table):
    return pl.pallas_call(
        gram_kernel,
        name="gram",
        out_shape=(
            jax.ShapeDtypeStruct((SUBS, LANES, FIELDS * LANES), BF16),
            jax.ShapeDtypeStruct((SUBS, LANES, FIELDS * LANES), BF16),
            jax.ShapeDtypeStruct(HALF, F32),
            jax.ShapeDtypeStruct(HALF, F32),
        ),
        in_specs=[vmem()] * 5 + [smem()],
        out_specs=(vmem(),) * 4,
        scratch_shapes=[pltpu.VMEM((SUBS, 2, ROWS, LANES), F32), pltpu.VMEM((ROWS, LANES), F32)],
        compiler_params=PARAMS,
    )(own, *near, weight16, table)


def run_factor(gram):
    return pl.pallas_call(
        factor_kernel,
        name="factor",
        out_shape=jax.ShapeDtypeStruct((2 * LANES, LANES), F32),
        in_specs=[vmem()],
        out_specs=vmem(),
        compiler_params=PARAMS,
    )(gram)


def run_modes(own, far, sh, sl, weights, table):
    return pl.pallas_call(
        modes_kernel,
        name="modes",
        out_shape=(
            jax.ShapeDtypeStruct((2, SUBS, ROWS, LANES), BF16),
            jax.ShapeDtypeStruct((2, SUBS, WIDTH, WIDTH), F32),
        ),
        in_specs=[vmem()] * 5 + [smem()],
        out_specs=(vmem(), vmem()),
        scratch_shapes=[
            pltpu.VMEM((2, 4, WIDTH, LANES), F32),
            pltpu.VMEM((2 * ROWS, LANES), F32),
            pltpu.VMEM((WIDTH, LANES), F32),
        ],
        compiler_params=PARAMS,
    )(own, far, sh, sl, weights, table)


def space_perm(along, shift):
    pairs = []
    for i in range(32):
        z, x, core = i // 8, i // 2 % 4, i % 2
        if along == "x":
            x = (x + shift) % 4
        elif along == "z":
            z = (z + shift) % 4
        else:
            core = 1 - core
        pairs.append((i, (z * 4 + x) * 2 + core))
    return pairs


def sum_over_chips(value):
    for along in ("x", "z"):
        far = [lax.ppermute(value, "space", space_perm(along, d)) for d in (1, 3, 2)]
        value = (value + far[2]) + (far[0] + far[1])
    return value


def on_device(spectra, weights):
    t = lax.axis_index("tm")
    flat = spectra.reshape(2, 2, 4, ROWS, LANES)
    own = lax.dynamic_index_in_dim(flat, t, 2, keepdims=False)
    near = []
    for d in range(1, 4):
        piece = lax.dynamic_index_in_dim(flat, (t + d) % 4, 2, keepdims=False)
        near.append(lax.ppermute(piece, "tm", [(i, (i + d) % 4) for i in range(4)]))
    weight16 = jnp.tile(weights, (4, 1))
    sh, sl, keep, send = run_gram(own, near, weight16, jnp.asarray(twiddle_table()))
    across = space_perm("core", 1)
    gram = sum_over_chips(keep + lax.ppermute(send, "space", across))
    factor = run_factor(gram)
    far = lax.ppermute(factor, "space", across)
    modes, upper = run_modes(factor, far, sh, sl, weights, jnp.asarray(phase_table()))
    return (
        modes.reshape(2, SUBS, 1, WIDTH, FIELDS, LANES),
        upper.reshape(2, SUBS, 1, WIDTH, WIDTH),
    )


def solution(mesh):
    placed = (P(None, "tm", None, None, None, "space"), P(None, "space"))
    return jax.shard_map(
        on_device,
        mesh=mesh,
        in_specs=placed,
        out_specs=(P(None, None, "tm", None, None, "space"), P(None, None, "tm", None, None)),
        check_vma=False,
    )
```

```python
import functools
import math

import jax
import jax.numpy as jnp
import numpy as np
from jax import lax
from jax.experimental import pallas as pl
from jax.experimental.pallas import tpu as pltpu
from jax.sharding import PartitionSpec as P

SUBS = 8
WIDTH = 64
FIELDS = 4
LANES = 128
ROWS = WIDTH * FIELDS
F32 = jnp.float32
BF16 = jnp.bfloat16


def by_bin(t, values):
    values = [float(v) for v in values]
    if len(set(values)) == 1:
        return F32(values[0])
    return jnp.where(
        t < 2, jnp.where(t == 0, values[0], values[1]), jnp.where(t == 2, values[2], values[3])
    ).astype(F32)


def unit(t, angles):
    return by_bin(t, np.cos(angles)), by_bin(t, np.sin(angles))


def source_twiddle(t, d):
    return unit(t, [-2.0 * math.pi * (((b - d) % 4) * b) / 16.0 for b in range(4)])


def second_twiddle(t, q):
    return unit(t, [-2.0 * math.pi * (b / 32.0 + q / 8.0) for b in range(4)])


def split(value):
    high = value.astype(BF16)
    return high, (value - high.astype(F32)).astype(BF16)


def lane_iota(shape):
    return lax.broadcasted_iota(jnp.int32, shape, len(shape) - 1)


SMALL = (8, LANES)


def places():
    lane = lane_iota(SMALL)
    sub = lax.broadcasted_iota(jnp.int32, SMALL, 0)
    parity = lane // WIDTH
    group = lane % 16
    return lane, sub, parity, group, group * 4 + sub % 4


def block_transpose(tiles):
    block = lane_iota(tiles[0].shape) // 16
    for bit in range(3):
        step = 1 << bit
        low = (block & step) == 0
        out = list(tiles)
        for x in range(8):
            if x & step == 0:
                y = x | step
                out[x] = jnp.where(low, tiles[x], pltpu.roll(tiles[y], 16 * step, 1))
                out[y] = jnp.where(low, pltpu.roll(tiles[x], LANES - 16 * step, 1), tiles[y])
        tiles = out
    return tiles


def gather_lanes(value, index):
    return jnp.take_along_axis(value, index, axis=1)


def reverse_rows(value, lane, sub):
    index = (1 - lane // WIDTH) * WIDTH + (lane % WIDTH) // 16 * 16 + 15 - lane % 16
    value = gather_lanes(value, index)
    value = jnp.where(sub % 2 == 0, pltpu.roll(value, 7, 0), pltpu.roll(value, 1, 0))
    return jnp.where(sub % 4 < 2, pltpu.roll(value, 6, 0), pltpu.roll(value, 2, 0))


def gram_kernel(own, near3, near1, near2, weight, sh_ref, sl_ref, keep_ref, send_ref, work, mixed):
    t = lax.axis_index("tm")
    root = jnp.sqrt(jnp.concatenate([weight[...]] * 4, axis=0))
    sources = (own, near1, near2, near3)
    tw = []
    for d in range(4):
        re, im = source_twiddle(t, d)
        tw.append((root * re, root * im))
    tq = [second_twiddle(t, q) for q in range(4)]

    def transform(step, _):
        row = pl.multiple_of(step * 16, 16)
        rows = pl.ds(row, 16)
        radix = []
        for s in range(2):
            y = []
            for d in range(4):
                re = sources[d][0, s, rows, :].astype(F32)
                im = sources[d][1, s, rows, :].astype(F32)
                y.append((re * tw[d][0] - im * tw[d][1], re * tw[d][1] + im * tw[d][0]))
            a = (y[0][0] + y[2][0], y[0][1] + y[2][1])
            b = (y[0][0] - y[2][0], y[0][1] - y[2][1])
            c = (y[1][0] + y[3][0], y[1][1] + y[3][1])
            e = (y[1][0] - y[3][0], y[1][1] - y[3][1])
            radix.append(
                [
                    (a[0] + c[0], a[1] + c[1]),
                    (b[0] - e[1], b[1] + e[0]),
                    (a[0] - c[0], a[1] - c[1]),
                    (b[0] + e[1], b[1] - e[0]),
                ]
            )
        for q in range(4):
            x0 = radix[0][q]
            x1 = radix[1][q]
            v = (x1[0] * tq[q][0] - x1[1] * tq[q][1], x1[0] * tq[q][1] + x1[1] * tq[q][0])
            work[q, 0, rows, :] = x0[0] + v[0]
            work[q, 1, rows, :] = x0[1] + v[1]
            work[q + 4, 0, rows, :] = x0[0] - v[0]
            work[q + 4, 1, rows, :] = x0[1] - v[1]
        return 0

    lax.fori_loop(0, ROWS // 16, transform, 0)

    left = lane_iota((WIDTH, LANES)) < WIDTH

    def one_gram(q):
        for part in range(2):
            for f in range(FIELDS):
                for s in range(4):
                    value = work[q, part, pl.ds(s * 4 + f, 16, stride=16), :]
                    high, low = split(value)
                    place = slice(part * WIDTH + s * 16, part * WIDTH + s * 16 + 16)
                    sh_ref[q, place, f * LANES : (f + 1) * LANES] = high
                    sl_ref[q, place, f * LANES : (f + 1) * LANES] = low
        high = sh_ref[q]
        both = jnp.concatenate([high, sl_ref[q]], axis=0)
        prod = lax.dot_general(both, high, (((1,), (1,)), ((), ())), preferred_element_type=F32)
        cross = prod[LANES:]
        full = prod[:LANES] + (cross + cross.T)
        low = pltpu.roll(full[WIDTH:], WIDTH, 1)
        return full[:WIDTH] + jnp.where(left, low, -low)

    lane, sub, parity, _, column = places()

    def half(base):
        tiles = [None] * 8
        for qq in range(4):
            tile = one_gram(base + qq)
            for p in range(2):
                tiles[p * 4 + qq] = jnp.concatenate(
                    [tile[p * 16 : p * 16 + 16], tile[32 + p * 16 : 48 + p * 16]], axis=0
                )
        for a, tile in enumerate(block_transpose(tiles)):
            mixed[a * 32 : (a + 1) * 32, :] = tile
        out = []
        for m in range(16):
            near = mixed[pl.ds(m % 2 * 16 + m // 2, 8, stride=32), :]
            far_m = 31 - m
            far = mixed[pl.ds(far_m % 2 * 16 + far_m // 2, 8, stride=32), :]
            far = reverse_rows(far, lane, sub)
            line = 2 * m + parity
            far = jnp.where(column == line, pltpu.roll(far, 4, 0), far)
            upper = (column > line) | ((column == line) & (sub < 4))
            out.append(jnp.where(upper, near, far))
        return out

    mine = lax.axis_index("space") % 2
    first = half(0)
    second = half(4)
    for m in range(16):
        keep_ref[m * 8 : (m + 1) * 8, :] = jnp.where(mine == 0, first[m], second[m])
        send_ref[m * 8 : (m + 1) * 8, :] = jnp.where(mine == 0, second[m], first[m])


def at_sub(value, index):
    return jnp.broadcast_to(value[index : index + 1, :], value.shape)


def factor_kernel(gram, out_ref):
    lane, sub, parity, group, column = places()
    first = parity == 0
    sign = jnp.where(sub < 4, 1.0, -1.0).astype(F32)
    real = sub < 4
    lane_base = lane // 16 * 16

    def turn(value):
        return pltpu.roll(value, 4, 0) * sign

    def lifted(value):
        return jnp.where(first, value, pltpu.roll(value, 7, 0))

    rows = [None] * 32
    for m in range(16):
        packed = gram[m * 8 : (m + 1) * 8, :]
        rows[m] = packed
        far = reverse_rows(packed, lane, sub)
        line = 2 * (31 - m) + parity
        rows[31 - m] = jnp.where(column == line, pltpu.roll(far, 4, 0), far)

    for g in range(16):
        pair = (rows[2 * g], rows[2 * g + 1])
        full, block, ahead = [], [], []
        for v in pair:
            turned = pltpu.roll(v, WIDTH, 1)
            one = jnp.where(first, v, turned)
            two = jnp.where(first, turned, v)
            full += [one, two]
            for p in range(2):
                block.append(gather_lanes(v, lane % WIDTH // 16 * 16 + p * WIDTH + g))
        if g < 15:
            for r in range(4):
                ahead.append(gather_lanes(lifted(full[r]), lane_base + g + 1))
        in_group = group == g
        inverse, root, scaled = [], [], []
        for s in range(4):
            here = in_group & (sub % 4 == s)
            pivot = at_sub(block[s], s)
            ip = 1.0 / pivot
            inverse.append(ip)
            root.append(lax.rsqrt(pivot))
            full[s] = jnp.where(here, jnp.where(real, 1.0, 0.0), full[s])
            y = full[s] * ip
            y_t = turn(y)
            b = block[s] * ip
            b_t = turn(b)
            if g < 15:
                n = ahead[s] * ip
                n_t = turn(n)
            for r in range(s + 1, 4):
                mr = at_sub(block[s], r)
                mi = at_sub(block[s], 4 + r)
                full[r] = jnp.where(here, 0.0, full[r]) - mr * y - mi * y_t
                block[r] = block[r] - mr * b - mi * b_t
                if g < 15:
                    ahead[r] = ahead[r] - mr * n - mi * n_t
            later = in_group & (sub % 4 > s)
            y = jnp.where(later, 0.0, y)
            scaled.append((y, jnp.where(later, 0.0, y_t)))
        raised = [lifted(full[r]) for r in range(4)]
        for h in range(g + 1, 16):
            if h == g + 1:
                multi = ahead
            else:
                multi = [gather_lanes(raised[r], lane_base + h) for r in range(4)]
            for odd in range(2):
                m = 2 * h + odd
                value = jnp.where(in_group, 0.0, rows[m])
                terms = []
                for r in range(4):
                    y, y_t = scaled[r]
                    terms.append(at_sub(multi[r], 2 * odd) * y + at_sub(multi[r], 4 + 2 * odd) * y_t)
                rows[m] = value - ((terms[0] + terms[1]) + (terms[2] + terms[3]))
        for odd in range(2):
            m = 2 * g + odd
            out_ref[m * 8 : (m + 1) * 8, :] = jnp.where(
                first, full[2 * odd] * root[2 * odd], full[2 * odd + 1] * root[2 * odd + 1]
            )


def modes_kernel(slot, *refs):
    if slot == 0:
        source, sh_ref, sl_ref, weight = refs[:4]
    else:
        source, sh_ref, sl_ref, weight, _, _ = refs[:6]
    modes_ref, upper_ref, turned, work, natural, modes_own, upper_own, modes_sem, upper_sem = refs[-9:]
    t = lax.axis_index("tm")
    mine = (lax.axis_index("space") + slot) % 2
    wide = (WIDTH, LANES)
    lane = lane_iota(wide)
    order = lax.broadcasted_iota(jnp.int32, wide, 0)
    line = order % 16 * 4 + order // 16 % 2 * 2 + order // 32
    column = lane % 16 * 4 + lane // 16 % 4
    left = lane < WIDTH
    lane8 = lane_iota(SMALL)
    natural_index = lane8 // WIDTH * WIDTH + lane8 % 4 * 16 + lane8 % WIDTH // 4
    root = lax.rsqrt(weight[...])

    tiles = []
    for a in range(8):
        tiles.append(
            jnp.concatenate(
                [source[pl.ds(a + 8 * odd, 16, stride=16), :] for odd in range(2)], axis=0
            )
        )
    for b, tile in enumerate(block_transpose(tiles)):
        turned[b % 4, b // 4 * 32 : b // 4 * 32 + 32, :] = tile

    copies = []
    for k in range(4):
        q = mine * 4 + k
        both = turned[k]
        inverse = jnp.where(column <= line, both, 0.0)
        diag = jnp.where(left, 1.0 / both, 0.0)
        upper = jnp.where(column > line, both, jnp.where(column == line, diag, 0.0))
        for j in range(4):
            s = 2 * (j % 2) + j // 2
            for h in range(2):
                piece = gather_lanes(upper[j * 16 + h * 8 : j * 16 + h * 8 + 8], natural_index)
                natural[k, pl.ds(s + 32 * h, 8, stride=4), :] = piece
        upper_own[0, k] = natural[k, :, :WIDTH]
        upper_own[1, k] = natural[k, :, WIDTH:]
        copies.append(
            pltpu.make_async_copy(upper_own.at[:, k], upper_ref.at[:, q], upper_sem.at[k])
        )
        copies[-1].start()
        swapped = pltpu.roll(inverse, WIDTH, 1)
        swapped = jnp.where(left, -swapped, swapped)
        pr = by_bin(t, [(1, 0, -1, 0)[b * k % 4] for b in range(4)])
        pi = by_bin(t, [(0, -1, 0, 1)[b * k % 4] for b in range(4)])
        lhs = jnp.concatenate([pr * inverse - pi * swapped, pr * swapped + pi * inverse], axis=0)
        lh, ll = split(lhs)
        sh = sh_ref[q]
        out = jnp.dot(lh, sh, preferred_element_type=F32)
        out = out + jnp.dot(ll, sh, preferred_element_type=F32)
        out = out + jnp.dot(lh, sl_ref[q], preferred_element_type=F32)
        for part in range(2):
            for f in range(FIELDS):
                block = out[part * WIDTH : (part + 1) * WIDTH, f * LANES : (f + 1) * LANES] * root[f : f + 1, :]
                for j in range(4):
                    s = 2 * (j % 2) + j // 2
                    work[k % 2, pl.ds(part * ROWS + s * 4 + f, 16, stride=16), :] = block[j * 16 : j * 16 + 16]
            modes_own[part, k] = work[k % 2, part * ROWS : (part + 1) * ROWS, :].astype(BF16)
        copies.append(
            pltpu.make_async_copy(modes_own.at[:, k], modes_ref.at[:, q], modes_sem.at[k])
        )
        copies[-1].start()
    for copy in copies:
        copy.wait()


def vmem():
    return pl.BlockSpec(memory_space=pltpu.VMEM)


HALF = (LANES, LANES)
ORDER = (3, 1, 2)
PARAMS = pltpu.CompilerParams(vmem_limit_bytes=32 * 1024 * 1024)


def run_gram(own, near, weights):
    return pl.pallas_call(
        gram_kernel,
        name="gram",
        out_shape=(
            jax.ShapeDtypeStruct((SUBS, LANES, FIELDS * LANES), BF16),
            jax.ShapeDtypeStruct((SUBS, LANES, FIELDS * LANES), BF16),
            jax.ShapeDtypeStruct(HALF, F32),
            jax.ShapeDtypeStruct(HALF, F32),
        ),
        in_specs=[vmem()] * 5,
        out_specs=(vmem(),) * 4,
        scratch_shapes=[pltpu.VMEM((SUBS, 2, ROWS, LANES), F32), pltpu.VMEM((ROWS, LANES), F32)],
        compiler_params=PARAMS,
    )(own, *near, weights)


def run_factor(gram):
    return pl.pallas_call(
        factor_kernel,
        name="factor",
        out_shape=jax.ShapeDtypeStruct((2 * LANES, LANES), F32),
        in_specs=[vmem()],
        out_specs=vmem(),
        compiler_params=PARAMS,
    )(gram)


def run_modes(slot, factor, sh, sl, weights, outputs=()):
    anywhere = pl.BlockSpec(memory_space=pl.ANY)
    return pl.pallas_call(
        functools.partial(modes_kernel, slot),
        name="modes_far" if slot else "modes_own",
        out_shape=(
            jax.ShapeDtypeStruct((2, SUBS, ROWS, LANES), BF16),
            jax.ShapeDtypeStruct((2, SUBS, WIDTH, WIDTH), F32),
        ),
        in_specs=[vmem()] * 4 + [anywhere] * len(outputs),
        out_specs=(anywhere, anywhere),
        scratch_shapes=[
            pltpu.VMEM((4, WIDTH, LANES), F32),
            pltpu.VMEM((2, 2 * ROWS, LANES), F32),
            pltpu.VMEM((4, WIDTH, LANES), F32),
            pltpu.VMEM((2, 4, ROWS, LANES), BF16),
            pltpu.VMEM((2, 4, WIDTH, WIDTH), F32),
            pltpu.SemaphoreType.DMA((4,)),
            pltpu.SemaphoreType.DMA((4,)),
        ],
        input_output_aliases={4: 0, 5: 1} if outputs else {},
        compiler_params=PARAMS,
        cost_estimate=pl.CostEstimate(flops=3 * 10**8, bytes_accessed=2**22, transcendentals=0),
    )(factor, sh, sl, weights, *outputs)


def space_perm(along, shift):
    pairs = []
    for i in range(32):
        z, x, core = i // 8, i // 2 % 4, i % 2
        if along == "x":
            x = (x + shift) % 4
        elif along == "z":
            z = (z + shift) % 4
        else:
            core = 1 - core
        pairs.append((i, (z * 4 + x) * 2 + core))
    return pairs


def sum_over_chips(value):
    for along in ("x", "z"):
        far = [lax.ppermute(value, "space", space_perm(along, d)) for d in (3, 1, 2)]
        value = ((value + far[0]) + far[1]) + far[2]
    return value


def on_device(spectra, weights):
    t = lax.axis_index("tm")
    flat = spectra.reshape(2, 2, 4, ROWS, LANES)

    def piece(d):
        source = lax.optimization_barrier(flat)
        return lax.dynamic_index_in_dim(source, (t + d) % 4, 2, keepdims=False)

    near = {}
    for d in ORDER:
        near[d] = lax.ppermute(piece(d), "tm", [(i, (i + d) % 4) for i in range(4)])
    own = piece(0)
    sh, sl, keep, send = run_gram(own, [near[d] for d in ORDER], weights)
    across = space_perm("core", 1)
    gram = sum_over_chips(keep + lax.ppermute(send, "space", across))
    factor = run_factor(gram)
    far = lax.ppermute(factor, "space", across)
    outputs = run_modes(0, factor, sh, sl, weights)
    modes, upper = run_modes(1, far, sh, sl, weights, outputs)
    return (
        modes.reshape(2, SUBS, 1, WIDTH, FIELDS, LANES),
        upper.reshape(2, SUBS, 1, WIDTH, WIDTH),
    )


def solution(mesh):
    placed = (P(None, "tm", None, None, None, "space"), P(None, "space"))
    return jax.shard_map(
        on_device,
        mesh=mesh,
        in_specs=placed,
        out_specs=(P(None, None, "tm", None, None, "space"), P(None, None, "tm", None, None)),
        check_vma=False,
    )
```

```python
import functools
import math

import jax
import jax.numpy as jnp
import numpy as np
from jax import lax
from jax.experimental import pallas as pl
from jax.experimental.pallas import tpu as pltpu
from jax.sharding import PartitionSpec as P

SUBS = 8
WIDTH = 64
FIELDS = 4
LANES = 128
ROWS = WIDTH * FIELDS
F32 = jnp.float32
BF16 = jnp.bfloat16


def by_bin(t, values):
    values = [float(v) for v in values]
    if len(set(values)) == 1:
        return F32(values[0])
    return jnp.where(
        t < 2, jnp.where(t == 0, values[0], values[1]), jnp.where(t == 2, values[2], values[3])
    ).astype(F32)


def unit(t, angles):
    return by_bin(t, np.cos(angles)), by_bin(t, np.sin(angles))


def source_twiddle(t, d):
    return unit(t, [-2.0 * math.pi * (((b - d) % 4) * b) / 16.0 for b in range(4)])


def second_twiddle(t, q):
    return unit(t, [-2.0 * math.pi * (b / 32.0 + q / 8.0) for b in range(4)])


def split(value):
    high = value.astype(BF16)
    return high, (value - high.astype(F32)).astype(BF16)


def lane_iota(shape):
    return lax.broadcasted_iota(jnp.int32, shape, len(shape) - 1)


SMALL = (8, LANES)


def places():
    lane = lane_iota(SMALL)
    sub = lax.broadcasted_iota(jnp.int32, SMALL, 0)
    parity = lane // WIDTH
    group = lane % 16
    return lane, sub, parity, group, group * 4 + sub % 4


def block_transpose(tiles):
    block = lane_iota(tiles[0].shape) // 16
    for bit in range(3):
        step = 1 << bit
        low = (block & step) == 0
        out = list(tiles)
        for x in range(8):
            if x & step == 0:
                y = x | step
                out[x] = jnp.where(low, tiles[x], pltpu.roll(tiles[y], 16 * step, 1))
                out[y] = jnp.where(low, pltpu.roll(tiles[x], LANES - 16 * step, 1), tiles[y])
        tiles = out
    return tiles


def gather_lanes(value, index):
    return jnp.take_along_axis(value, index, axis=1)


def reverse_rows(value, lane, sub):
    index = (1 - lane // WIDTH) * WIDTH + (lane % WIDTH) // 16 * 16 + 15 - lane % 16
    value = gather_lanes(value, index)
    value = jnp.where(sub % 2 == 0, pltpu.roll(value, 7, 0), pltpu.roll(value, 1, 0))
    return jnp.where(sub % 4 < 2, pltpu.roll(value, 6, 0), pltpu.roll(value, 2, 0))


def pack_gram(work, s_ref, out_ref, mixed, products):
    left = lane_iota((WIDTH, LANES)) < WIDTH
    for q in range(4):
        for part in range(2):
            for f in range(FIELDS):
                for j in range(4):
                    value = work[q, part, pl.ds(j * 4 + f, 16, stride=16), :]
                    high, low = split(value)
                    row = part * WIDTH + j * 16
                    s_ref[q, row : row + 16, f * LANES : (f + 1) * LANES] = high
                    s_ref[q, LANES + row : LANES + row + 16, f * LANES : (f + 1) * LANES] = low

    for q in range(4):
        products[q] = lax.dot_general(
            s_ref[q], s_ref[q, :LANES], (((1,), (1,)), ((), ())), preferred_element_type=F32
        )

    tiles = [None] * 8
    for q in range(4):
        cross = products[q, LANES:]
        full = products[q, :LANES] + (cross + cross.T)
        low = pltpu.roll(full[WIDTH:], WIDTH, 1)
        tile = full[:WIDTH] + jnp.where(left, low, -low)
        for p in range(2):
            tiles[p * 4 + q] = jnp.concatenate(
                [tile[p * 16 : p * 16 + 16], tile[32 + p * 16 : 48 + p * 16]], axis=0
            )
    for a, tile in enumerate(block_transpose(tiles)):
        mixed[a * 32 : (a + 1) * 32, :] = tile
    lane, sub, parity, _, column = places()
    for m in range(16):
        near = mixed[pl.ds(m % 2 * 16 + m // 2, 8, stride=32), :]
        far_m = 31 - m
        far = mixed[pl.ds(far_m % 2 * 16 + far_m // 2, 8, stride=32), :]
        far = reverse_rows(far, lane, sub)
        line = 2 * m + parity
        far = jnp.where(column == line, pltpu.roll(far, 4, 0), far)
        upper = (column > line) | ((column == line) & (sub < 4))
        out_ref[m * 8 : (m + 1) * 8, :] = jnp.where(upper, near, far)


def send_kernel(own, near3, near1, near2, weight, other_ref, s_ref, send_ref, work, mixed, products):
    t = lax.axis_index("tm")
    side = jnp.where(lax.axis_index("space") % 2 == 0, -1.0, 1.0).astype(F32)
    root = jnp.sqrt(jnp.concatenate([weight[...]] * 4, axis=0))
    sources = (own, near1, near2, near3)
    tw = []
    for d in range(4):
        re, im = source_twiddle(t, d)
        tw.append((root * re, root * im))
    tq = []
    for q in range(4):
        re, im = second_twiddle(t, q)
        tq.append((re * side, im * side))

    def transform(step, _):
        row = pl.multiple_of(step * 16, 16)
        rows = pl.ds(row, 16)
        radix = []
        for s in range(2):
            y = []
            for d in range(4):
                re = sources[d][0, s, rows, :].astype(F32)
                im = sources[d][1, s, rows, :].astype(F32)
                y.append((re * tw[d][0] - im * tw[d][1], re * tw[d][1] + im * tw[d][0]))
            a = (y[0][0] + y[2][0], y[0][1] + y[2][1])
            b = (y[0][0] - y[2][0], y[0][1] - y[2][1])
            c = (y[1][0] + y[3][0], y[1][1] + y[3][1])
            e = (y[1][0] - y[3][0], y[1][1] - y[3][1])
            radix.append(
                [
                    (a[0] + c[0], a[1] + c[1]),
                    (b[0] - e[1], b[1] + e[0]),
                    (a[0] - c[0], a[1] - c[1]),
                    (b[0] + e[1], b[1] - e[0]),
                ]
            )
        for q in range(4):
            x0 = radix[0][q]
            x1 = radix[1][q]
            v = (x1[0] * tq[q][0] - x1[1] * tq[q][1], x1[0] * tq[q][1] + x1[1] * tq[q][0])
            work[q, 0, rows, :] = x0[0] + v[0]
            work[q, 1, rows, :] = x0[1] + v[1]
            other_ref[q, 0, rows, :] = x0[0] - v[0]
            other_ref[q, 1, rows, :] = x0[1] - v[1]
        return 0

    lax.fori_loop(0, ROWS // 16, transform, 0)
    pack_gram(work, s_ref, send_ref, mixed, products)


def at_sub(value, index):
    return jnp.broadcast_to(value[index : index + 1, :], value.shape)


def factor_kernel(gram, out_ref, spread):
    lane, sub, parity, group, column = places()
    first = parity == 0
    sign = jnp.where(sub < 4, 1.0, -1.0).astype(F32)
    real = sub < 4
    lane_base = lane // 16 * 16

    def turn(value):
        return pltpu.roll(value, 4, 0) * sign

    def lifted(value):
        return jnp.where(first, value, pltpu.roll(value, 7, 0))

    rows = [None] * 32
    for m in range(16):
        packed = gram[m * 8 : (m + 1) * 8, :]
        rows[m] = packed
        far = reverse_rows(packed, lane, sub)
        line = 2 * (31 - m) + parity
        rows[31 - m] = jnp.where(column == line, pltpu.roll(far, 4, 0), far)

    def block_of(v, p, g):
        return gather_lanes(v, lane % WIDTH // 16 * 16 + p * WIDTH + g)

    block = [block_of(rows[r // 2], r % 2, 0) for r in range(4)]
    for g in range(16):
        last = g == 15
        full, ahead, following = [], [], []
        for v in (rows[2 * g], rows[2 * g + 1]):
            turned = pltpu.roll(v, WIDTH, 1)
            full += [jnp.where(first, v, turned), jnp.where(first, turned, v)]
        if not last:
            ahead = [block_of(rows[2 * g + r // 2], r % 2, g + 1) for r in range(4)]
            following = [block_of(rows[2 * g + 2 + r // 2], r % 2, g + 1) for r in range(4)]
        in_group = group == g
        root, scaled = [], []
        for s in range(4):
            here = in_group & (sub % 4 == s)
            pivot = at_sub(block[s], s)
            ip = 1.0 / pivot
            root.append(lax.rsqrt(pivot))
            full[s] = jnp.where(here, jnp.where(real, 1.0, 0.0), full[s])
            y = full[s] * ip
            y_t = turn(y)
            b = block[s] * ip
            b_t = turn(b)
            if not last:
                n = ahead[s] * ip
                n_t = turn(n)
                for r in range(4):
                    mr = at_sub(ahead[s], r)
                    mi = at_sub(ahead[s], 4 + r)
                    following[r] = following[r] - (mr * n + mi * n_t)
            for r in range(s + 1, 4):
                mr = at_sub(block[s], r)
                mi = at_sub(block[s], 4 + r)
                full[r] = jnp.where(here, 0.0, full[r]) - (mr * y + mi * y_t)
                block[r] = block[r] - (mr * b + mi * b_t)
                if not last:
                    ahead[r] = ahead[r] - (mr * n + mi * n_t)
            later = in_group & (sub % 4 > s)
            scaled.append((jnp.where(later, 0.0, y), jnp.where(later, 0.0, y_t)))
        raised = [lifted(full[r]) for r in range(4)]
        for h in range(g + 1, 16):
            if h == g + 1:
                multi = [lifted(ahead[r]) for r in range(4)]
            else:
                multi = [gather_lanes(raised[r], lane_base + h) for r in range(4)]
            for odd in range(2):
                m = 2 * h + odd
                value = jnp.where(in_group, 0.0, rows[m])
                terms = []
                for r in range(4):
                    y, y_t = scaled[r]
                    terms.append(at_sub(multi[r], 2 * odd) * y + at_sub(multi[r], 4 + 2 * odd) * y_t)
                rows[m] = value - ((terms[0] + terms[1]) + (terms[2] + terms[3]))
        block = following
        for odd in range(2):
            m = 2 * g + odd
            spread[m * 8 : (m + 1) * 8, :] = jnp.where(
                first, full[2 * odd] * root[2 * odd], full[2 * odd + 1] * root[2 * odd + 1]
            )
        if g % 4 == 3:
            k = g // 4
            tiles = [spread[pl.ds(k * WIDTH + a, 8, stride=8), :] for a in range(8)]
            for b, tile in enumerate(block_transpose(tiles)):
                row = b // 4 * 32 + k * 8
                out_ref[b % 4, row : row + 8, :] = tile


def modes_kernel(slot, *refs):
    if slot == 0:
        source, s_ref, weight = refs[:3]
    else:
        source, s_ref, weight, _, _ = refs[:5]
    modes_ref, upper_ref, work, natural, modes_own, upper_own, modes_sem, upper_sem = refs[-8:]
    t = lax.axis_index("tm")
    mine = (lax.axis_index("space") + slot) % 2
    wide = (WIDTH, LANES)
    lane = lane_iota(wide)
    order = lax.broadcasted_iota(jnp.int32, wide, 0)
    line = order % 32 * 2 + order // 32
    column = lane % 16 * 4 + lane // 16 % 4
    left = lane < WIDTH
    lane8 = lane_iota(SMALL)
    natural_index = lane8 // WIDTH * WIDTH + lane8 % 4 * 16 + lane8 % WIDTH // 4
    root = lax.rsqrt(weight[...])

    copies = []
    for k in range(4):
        q = mine * 4 + k
        both = source[k]
        inverse = jnp.where(column <= line, both, 0.0)
        diag = jnp.where(left, 1.0 / both, 0.0)
        upper = jnp.where(column > line, both, jnp.where(column == line, diag, 0.0))
        for j in range(8):
            piece = gather_lanes(upper[j * 8 : j * 8 + 8], natural_index)
            natural[k, pl.ds(j // 4 + j % 4 * 16, 8, stride=2), :] = piece
        upper_own[0, k] = natural[k, :, :WIDTH]
        upper_own[1, k] = natural[k, :, WIDTH:]
        copies.append(
            pltpu.make_async_copy(upper_own.at[:, k], upper_ref.at[:, q], upper_sem.at[k])
        )
        copies[-1].start()
        swapped = pltpu.roll(inverse, WIDTH, 1)
        swapped = jnp.where(left, -swapped, swapped)
        pr = by_bin(t, [(1, 0, -1, 0)[b * k % 4] for b in range(4)])
        pi = by_bin(t, [(0, -1, 0, 1)[b * k % 4] for b in range(4)])
        lhs = jnp.concatenate([pr * inverse - pi * swapped, pr * swapped + pi * inverse], axis=0)
        lh, ll = split(lhs)
        out = jnp.dot(jnp.concatenate([lh, lh], axis=1), s_ref[k], preferred_element_type=F32)
        out = out + jnp.dot(ll, s_ref[k, :LANES], preferred_element_type=F32)
        for part in range(2):
            for f in range(FIELDS):
                for p in range(2):
                    row = part * WIDTH + p * 32
                    block = out[row : row + 32, f * LANES : (f + 1) * LANES] * root[f : f + 1, :]
                    work[k % 2, pl.ds(part * ROWS + p * 4 + f, 32, stride=8), :] = block
            modes_own[part, k] = work[k % 2, part * ROWS : (part + 1) * ROWS, :].astype(BF16)
        copies.append(
            pltpu.make_async_copy(modes_own.at[:, k], modes_ref.at[:, q], modes_sem.at[k])
        )
        copies[-1].start()
    for copy in copies:
        copy.wait()


def vmem():
    return pl.BlockSpec(memory_space=pltpu.VMEM)


HALF = (LANES, LANES)
ORDER = (3, 1, 2)
PARAMS = pltpu.CompilerParams(vmem_limit_bytes=32 * 1024 * 1024)


def run_send(own, near, weights):
    return pl.pallas_call(
        send_kernel,
        name="send_gram",
        out_shape=(
            jax.ShapeDtypeStruct((4, 2, ROWS, LANES), F32),
            jax.ShapeDtypeStruct((4, 2 * LANES, FIELDS * LANES), BF16),
            jax.ShapeDtypeStruct(HALF, F32),
        ),
        in_specs=[vmem()] * 5,
        out_specs=(vmem(),) * 3,
        scratch_shapes=[
            pltpu.VMEM((4, 2, ROWS, LANES), F32),
            pltpu.VMEM((ROWS, LANES), F32),
            pltpu.VMEM((4, 2 * LANES, LANES), F32),
        ],
        compiler_params=PARAMS,
    )(own, *near, weights)


def run_keep(work):
    return pl.pallas_call(
        pack_gram,
        name="keep_gram",
        out_shape=(
            jax.ShapeDtypeStruct((4, 2 * LANES, FIELDS * LANES), BF16),
            jax.ShapeDtypeStruct(HALF, F32),
        ),
        in_specs=[vmem()],
        out_specs=(vmem(),) * 2,
        scratch_shapes=[
            pltpu.VMEM((ROWS, LANES), F32),
            pltpu.VMEM((4, 2 * LANES, LANES), F32),
        ],
        compiler_params=PARAMS,
        cost_estimate=pl.CostEstimate(flops=3 * 10**8, bytes_accessed=2**21, transcendentals=0),
    )(work)


def run_factor(gram):
    return pl.pallas_call(
        factor_kernel,
        name="factor",
        out_shape=jax.ShapeDtypeStruct((4, WIDTH, LANES), F32),
        in_specs=[vmem()],
        out_specs=vmem(),
        scratch_shapes=[pltpu.VMEM((2 * LANES, LANES), F32)],
        compiler_params=PARAMS,
    )(gram)


def run_modes(slot, factor, s, weights, outputs=()):
    anywhere = pl.BlockSpec(memory_space=pl.ANY)
    return pl.pallas_call(
        functools.partial(modes_kernel, slot),
        name="modes_far" if slot else "modes_own",
        out_shape=(
            jax.ShapeDtypeStruct((2, SUBS, ROWS, LANES), BF16),
            jax.ShapeDtypeStruct((2, SUBS, WIDTH, WIDTH), F32),
        ),
        in_specs=[vmem()] * 3 + [anywhere] * len(outputs),
        out_specs=(anywhere, anywhere),
        scratch_shapes=[
            pltpu.VMEM((2, 2 * ROWS, LANES), F32),
            pltpu.VMEM((4, WIDTH, LANES), F32),
            pltpu.VMEM((2, 4, ROWS, LANES), BF16),
            pltpu.VMEM((2, 4, WIDTH, WIDTH), F32),
            pltpu.SemaphoreType.DMA((4,)),
            pltpu.SemaphoreType.DMA((4,)),
        ],
        input_output_aliases={3: 0, 4: 1} if outputs else {},
        compiler_params=PARAMS,
        cost_estimate=pl.CostEstimate(flops=3 * 10**8, bytes_accessed=2**22, transcendentals=0),
    )(factor, s, weights, *outputs)


def space_perm(along, shift):
    pairs = []
    for i in range(32):
        z, x, core = i // 8, i // 2 % 4, i % 2
        if along == "x":
            x = (x + shift) % 4
        elif along == "z":
            z = (z + shift) % 4
        else:
            core = 1 - core
        pairs.append((i, (z * 4 + x) * 2 + core))
    return pairs


def sum_over_chips(value):
    for along in ("x", "z"):
        far = [lax.ppermute(value, "space", space_perm(along, d)) for d in (3, 1, 2)]
        value = ((value + far[0]) + far[1]) + far[2]
    return value


def on_device(spectra, weights):
    t = lax.axis_index("tm")
    flat = spectra.reshape(2, 2, 4, ROWS, LANES)

    def piece(d):
        source = lax.optimization_barrier(flat)
        return lax.dynamic_index_in_dim(source, (t + d) % 4, 2, keepdims=False)

    near = {}
    for d in ORDER:
        near[d] = lax.ppermute(piece(d), "tm", [(i, (i + d) % 4) for i in range(4)])
    own = piece(0)
    other, s_far, send = run_send(own, [near[d] for d in ORDER], weights)
    across = space_perm("core", 1)
    arrived = lax.ppermute(send, "space", across)
    s_own, keep = run_keep(other)
    gram = sum_over_chips(keep + arrived)
    factor = run_factor(gram)
    far = lax.ppermute(factor, "space", across)
    outputs = run_modes(0, factor, s_own, weights)
    modes, upper = run_modes(1, far, s_far, weights, outputs)
    return (
        modes.reshape(2, SUBS, 1, WIDTH, FIELDS, LANES),
        upper.reshape(2, SUBS, 1, WIDTH, WIDTH),
    )


def solution(mesh):
    placed = (P(None, "tm", None, None, None, "space"), P(None, "space"))
    return jax.shard_map(
        on_device,
        mesh=mesh,
        in_specs=placed,
        out_specs=(P(None, None, "tm", None, None, "space"), P(None, None, "tm", None, None)),
        check_vma=False,
    )
```

```python
import functools
import math

import jax
import jax.numpy as jnp
import numpy as np
from jax import lax
from jax.experimental import pallas as pl
from jax.experimental.pallas import tpu as pltpu
from jax.sharding import PartitionSpec as P

SUBS = 8
WIDTH = 64
FIELDS = 4
LANES = 128
ROWS = WIDTH * FIELDS
F32 = jnp.float32
BF16 = jnp.bfloat16


def by_bin(t, values):
    values = [float(v) for v in values]
    if len(set(values)) == 1:
        return F32(values[0])
    return jnp.where(
        t < 2, jnp.where(t == 0, values[0], values[1]), jnp.where(t == 2, values[2], values[3])
    ).astype(F32)


def unit(t, angles):
    return by_bin(t, np.cos(angles)), by_bin(t, np.sin(angles))


def source_twiddle(t, d):
    return unit(t, [-2.0 * math.pi * (((b - d) % 4) * b) / 16.0 for b in range(4)])


def second_twiddle(t, q):
    return unit(t, [-2.0 * math.pi * (b / 32.0 + q / 8.0) for b in range(4)])


def split(value):
    high = value.astype(BF16)
    return high, (value - high.astype(F32)).astype(BF16)


def lane_iota(shape):
    return lax.broadcasted_iota(jnp.int32, shape, len(shape) - 1)


SMALL = (8, LANES)


def places():
    lane = lane_iota(SMALL)
    sub = lax.broadcasted_iota(jnp.int32, SMALL, 0)
    parity = lane // WIDTH
    group = lane % 16
    return lane, sub, parity, group, group * 4 + sub % 4


def block_transpose(tiles):
    block = lane_iota(tiles[0].shape) // 16
    for bit in range(3):
        step = 1 << bit
        low = (block & step) == 0
        out = list(tiles)
        for x in range(8):
            if x & step == 0:
                y = x | step
                out[x] = jnp.where(low, tiles[x], pltpu.roll(tiles[y], 16 * step, 1))
                out[y] = jnp.where(low, pltpu.roll(tiles[x], LANES - 16 * step, 1), tiles[y])
        tiles = out
    return tiles


def gather_lanes(value, index):
    return jnp.take_along_axis(value, index, axis=1)


def reverse_rows(value, lane, sub):
    index = (1 - lane // WIDTH) * WIDTH + (lane % WIDTH) // 16 * 16 + 15 - lane % 16
    value = gather_lanes(value, index)
    value = jnp.where(sub % 2 == 0, pltpu.roll(value, 7, 0), pltpu.roll(value, 1, 0))
    return jnp.where(sub % 4 < 2, pltpu.roll(value, 6, 0), pltpu.roll(value, 2, 0))


def pack_gram(work, s_ref, out_ref, mixed, products):
    left = lane_iota((WIDTH, LANES)) < WIDTH
    for q in range(4):
        for part in range(2):
            for f in range(FIELDS):
                for j in range(4):
                    value = work[q, part, pl.ds(j * 4 + f, 16, stride=16), :]
                    high, low = split(value)
                    row = part * WIDTH + j * 16
                    s_ref[q, row : row + 16, f * LANES : (f + 1) * LANES] = high
                    s_ref[q, LANES + row : LANES + row + 16, f * LANES : (f + 1) * LANES] = low

    for q in range(4):
        products[q] = lax.dot_general(
            s_ref[q], s_ref[q, :LANES], (((1,), (1,)), ((), ())), preferred_element_type=F32
        )

    tiles = [None] * 8
    for q in range(4):
        cross = products[q, LANES:]
        full = products[q, :LANES] + (cross + cross.T)
        low = pltpu.roll(full[WIDTH:], WIDTH, 1)
        tile = full[:WIDTH] + jnp.where(left, low, -low)
        for p in range(2):
            tiles[p * 4 + q] = jnp.concatenate(
                [tile[p * 16 : p * 16 + 16], tile[32 + p * 16 : 48 + p * 16]], axis=0
            )
    for a, tile in enumerate(block_transpose(tiles)):
        mixed[a * 32 : (a + 1) * 32, :] = tile
    lane, sub, parity, _, column = places()
    for m in range(16):
        near = mixed[pl.ds(m % 2 * 16 + m // 2, 8, stride=32), :]
        far_m = 31 - m
        far = mixed[pl.ds(far_m % 2 * 16 + far_m // 2, 8, stride=32), :]
        far = reverse_rows(far, lane, sub)
        line = 2 * m + parity
        far = jnp.where(column == line, pltpu.roll(far, 4, 0), far)
        upper = (column > line) | ((column == line) & (sub < 4))
        out_ref[m * 8 : (m + 1) * 8, :] = jnp.where(upper, near, far)


def twiddles(weight, shifts):
    t = lax.axis_index("tm")
    root = jnp.sqrt(jnp.concatenate([weight[...]] * 4, axis=0))
    out = []
    for d in shifts:
        re, im = source_twiddle(t, d)
        out.append((root * re, root * im))
    return out


def twisted(source, s, rows, tw):
    re = source[0, s, rows, :].astype(F32)
    im = source[1, s, rows, :].astype(F32)
    return re * tw[0] - im * tw[1], re * tw[1] + im * tw[0]


def even_kernel(own, near2, weight, even_ref):
    tw = twiddles(weight, (0, 2))

    def step(index, _):
        rows = pl.ds(pl.multiple_of(index * 16, 16), 16)
        for s in range(2):
            y0 = twisted(own, s, rows, tw[0])
            y2 = twisted(near2, s, rows, tw[1])
            even_ref[s, 0, rows, :] = y0[0] + y2[0]
            even_ref[s, 1, rows, :] = y0[1] + y2[1]
            even_ref[s, 2, rows, :] = y0[0] - y2[0]
            even_ref[s, 3, rows, :] = y0[1] - y2[1]
        return 0

    lax.fori_loop(0, ROWS // 16, step, 0)


def send_kernel(near3, near1, weight, even, other_ref, s_ref, send_ref, work, mixed, products):
    t = lax.axis_index("tm")
    side = jnp.where(lax.axis_index("space") % 2 == 0, -1.0, 1.0).astype(F32)
    tw = twiddles(weight, (1, 3))
    tq = []
    for q in range(4):
        re, im = second_twiddle(t, q)
        tq.append((re * side, im * side))

    def step(index, _):
        rows = pl.ds(pl.multiple_of(index * 16, 16), 16)
        radix = []
        for s in range(2):
            y1 = twisted(near1, s, rows, tw[0])
            y3 = twisted(near3, s, rows, tw[1])
            a = (even[s, 0, rows, :], even[s, 1, rows, :])
            b = (even[s, 2, rows, :], even[s, 3, rows, :])
            c = (y1[0] + y3[0], y1[1] + y3[1])
            e = (y1[0] - y3[0], y1[1] - y3[1])
            radix.append(
                [
                    (a[0] + c[0], a[1] + c[1]),
                    (b[0] - e[1], b[1] + e[0]),
                    (a[0] - c[0], a[1] - c[1]),
                    (b[0] + e[1], b[1] - e[0]),
                ]
            )
        for q in range(4):
            x0 = radix[0][q]
            x1 = radix[1][q]
            v = (x1[0] * tq[q][0] - x1[1] * tq[q][1], x1[0] * tq[q][1] + x1[1] * tq[q][0])
            work[q, 0, rows, :] = x0[0] + v[0]
            work[q, 1, rows, :] = x0[1] + v[1]
            other_ref[q, 0, rows, :] = x0[0] - v[0]
            other_ref[q, 1, rows, :] = x0[1] - v[1]
        return 0

    lax.fori_loop(0, ROWS // 16, step, 0)
    pack_gram(work, s_ref, send_ref, mixed, products)


def at_sub(value, index):
    return jnp.broadcast_to(value[index : index + 1, :], value.shape)


def factor_kernel(gram, out_ref, spread):
    lane, sub, parity, group, column = places()
    first = parity == 0
    sign = jnp.where(sub < 4, 1.0, -1.0).astype(F32)
    real = sub < 4
    lane_base = lane // 16 * 16

    def turn(value):
        return pltpu.roll(value, 4, 0) * sign

    def lifted(value):
        return jnp.where(first, value, pltpu.roll(value, 7, 0))

    rows = [None] * 32
    for m in range(16):
        packed = gram[m * 8 : (m + 1) * 8, :]
        rows[m] = packed
        far = reverse_rows(packed, lane, sub)
        line = 2 * (31 - m) + parity
        rows[31 - m] = jnp.where(column == line, pltpu.roll(far, 4, 0), far)

    def block_of(v, p, g):
        return gather_lanes(v, lane % WIDTH // 16 * 16 + p * WIDTH + g)

    block = [block_of(rows[r // 2], r % 2, 0) for r in range(4)]
    for g in range(16):
        last = g == 15
        full, ahead, following = [], [], []
        for v in (rows[2 * g], rows[2 * g + 1]):
            turned = pltpu.roll(v, WIDTH, 1)
            full += [jnp.where(first, v, turned), jnp.where(first, turned, v)]
        if not last:
            ahead = [block_of(rows[2 * g + r // 2], r % 2, g + 1) for r in range(4)]
            following = [block_of(rows[2 * g + 2 + r // 2], r % 2, g + 1) for r in range(4)]
        in_group = group == g
        root, scaled = [], []
        for s in range(4):
            here = in_group & (sub % 4 == s)
            pivot = at_sub(block[s], s)
            ip = 1.0 / pivot
            root.append(lax.rsqrt(pivot))
            full[s] = jnp.where(here, jnp.where(real, 1.0, 0.0), full[s])
            y = full[s] * ip
            y_t = turn(y)
            b = block[s] * ip
            b_t = turn(b)
            if not last:
                n = ahead[s] * ip
                n_t = turn(n)
                for r in range(4):
                    mr = at_sub(ahead[s], r)
                    mi = at_sub(ahead[s], 4 + r)
                    following[r] = following[r] - (mr * n + mi * n_t)
            for r in range(s + 1, 4):
                mr = at_sub(block[s], r)
                mi = at_sub(block[s], 4 + r)
                full[r] = jnp.where(here, 0.0, full[r]) - (mr * y + mi * y_t)
                block[r] = block[r] - (mr * b + mi * b_t)
                if not last:
                    ahead[r] = ahead[r] - (mr * n + mi * n_t)
            later = in_group & (sub % 4 > s)
            scaled.append((jnp.where(later, 0.0, y), jnp.where(later, 0.0, y_t)))
        raised = [lifted(full[r]) for r in range(4)]
        for h in range(g + 1, 16):
            if h == g + 1:
                multi = [lifted(ahead[r]) for r in range(4)]
            else:
                multi = [gather_lanes(raised[r], lane_base + h) for r in range(4)]
            for odd in range(2):
                m = 2 * h + odd
                value = jnp.where(in_group, 0.0, rows[m])
                terms = []
                for r in range(4):
                    y, y_t = scaled[r]
                    terms.append(at_sub(multi[r], 2 * odd) * y + at_sub(multi[r], 4 + 2 * odd) * y_t)
                rows[m] = value - ((terms[0] + terms[1]) + (terms[2] + terms[3]))
        block = following
        for odd in range(2):
            m = 2 * g + odd
            spread[m * 8 : (m + 1) * 8, :] = jnp.where(
                first, full[2 * odd] * root[2 * odd], full[2 * odd + 1] * root[2 * odd + 1]
            )
        if g % 4 == 3:
            k = g // 4
            tiles = [spread[pl.ds(k * WIDTH + a, 8, stride=8), :] for a in range(8)]
            for b, tile in enumerate(block_transpose(tiles)):
                row = b // 4 * 32 + k * 8
                out_ref[b % 4, row : row + 8, :] = tile


def modes_kernel(slot, *refs):
    if slot == 0:
        source, s_ref, weight = refs[:3]
    else:
        source, s_ref, weight, _, _ = refs[:5]
    modes_ref, upper_ref, work, natural, modes_own, upper_own, modes_sem, upper_sem = refs[-8:]
    t = lax.axis_index("tm")
    mine = (lax.axis_index("space") + slot) % 2
    wide = (WIDTH, LANES)
    lane = lane_iota(wide)
    order = lax.broadcasted_iota(jnp.int32, wide, 0)
    line = order % 32 * 2 + order // 32
    column = lane % 16 * 4 + lane // 16 % 4
    left = lane < WIDTH
    lane8 = lane_iota(SMALL)
    natural_index = lane8 // WIDTH * WIDTH + lane8 % 4 * 16 + lane8 % WIDTH // 4
    root = lax.rsqrt(weight[...])

    copies = []
    for k in range(4):
        q = mine * 4 + k
        both = source[k]
        inverse = jnp.where(column <= line, both, 0.0)
        diag = jnp.where(left, 1.0 / both, 0.0)
        upper = jnp.where(column > line, both, jnp.where(column == line, diag, 0.0))
        for j in range(8):
            piece = gather_lanes(upper[j * 8 : j * 8 + 8], natural_index)
            natural[k, pl.ds(j // 4 + j % 4 * 16, 8, stride=2), :] = piece
        upper_own[0, k] = natural[k, :, :WIDTH]
        upper_own[1, k] = natural[k, :, WIDTH:]
        copies.append(
            pltpu.make_async_copy(upper_own.at[:, k], upper_ref.at[:, q], upper_sem.at[k])
        )
        copies[-1].start()
        swapped = pltpu.roll(inverse, WIDTH, 1)
        swapped = jnp.where(left, -swapped, swapped)
        pr = by_bin(t, [(1, 0, -1, 0)[b * k % 4] for b in range(4)])
        pi = by_bin(t, [(0, -1, 0, 1)[b * k % 4] for b in range(4)])
        lhs = jnp.concatenate([pr * inverse - pi * swapped, pr * swapped + pi * inverse], axis=0)
        lh, ll = split(lhs)
        out = jnp.dot(jnp.concatenate([lh, lh], axis=1), s_ref[k], preferred_element_type=F32)
        out = out + jnp.dot(ll, s_ref[k, :LANES], preferred_element_type=F32)
        for part in range(2):
            for f in range(FIELDS):
                for p in range(2):
                    row = part * WIDTH + p * 32
                    block = out[row : row + 32, f * LANES : (f + 1) * LANES] * root[f : f + 1, :]
                    work[k % 2, pl.ds(part * ROWS + p * 4 + f, 32, stride=8), :] = block
            modes_own[part, k] = work[k % 2, part * ROWS : (part + 1) * ROWS, :].astype(BF16)
        copies.append(
            pltpu.make_async_copy(modes_own.at[:, k], modes_ref.at[:, q], modes_sem.at[k])
        )
        copies[-1].start()
    for copy in copies:
        copy.wait()


def vmem():
    return pl.BlockSpec(memory_space=pltpu.VMEM)


HALF = (LANES, LANES)
PARAMS = pltpu.CompilerParams(vmem_limit_bytes=32 * 1024 * 1024)


def run_even(own, near2, weights):
    return pl.pallas_call(
        even_kernel,
        name="even",
        out_shape=jax.ShapeDtypeStruct((2, 4, ROWS, LANES), F32),
        in_specs=[vmem()] * 3,
        out_specs=vmem(),
        compiler_params=PARAMS,
        cost_estimate=pl.CostEstimate(flops=2**22, bytes_accessed=2**21, transcendentals=0),
    )(own, near2, weights)


def run_send(near3, near1, weights, even):
    return pl.pallas_call(
        send_kernel,
        name="send_gram",
        out_shape=(
            jax.ShapeDtypeStruct((4, 2, ROWS, LANES), F32),
            jax.ShapeDtypeStruct((4, 2 * LANES, FIELDS * LANES), BF16),
            jax.ShapeDtypeStruct(HALF, F32),
        ),
        in_specs=[vmem()] * 4,
        out_specs=(vmem(),) * 3,
        scratch_shapes=[
            pltpu.VMEM((4, 2, ROWS, LANES), F32),
            pltpu.VMEM((ROWS, LANES), F32),
            pltpu.VMEM((4, 2 * LANES, LANES), F32),
        ],
        compiler_params=PARAMS,
    )(near3, near1, weights, even)


def run_keep(work):
    return pl.pallas_call(
        pack_gram,
        name="keep_gram",
        out_shape=(
            jax.ShapeDtypeStruct((4, 2 * LANES, FIELDS * LANES), BF16),
            jax.ShapeDtypeStruct(HALF, F32),
        ),
        in_specs=[vmem()],
        out_specs=(vmem(),) * 2,
        scratch_shapes=[
            pltpu.VMEM((ROWS, LANES), F32),
            pltpu.VMEM((4, 2 * LANES, LANES), F32),
        ],
        compiler_params=PARAMS,
        cost_estimate=pl.CostEstimate(flops=3 * 10**8, bytes_accessed=2**21, transcendentals=0),
    )(work)


def run_factor(gram):
    return pl.pallas_call(
        factor_kernel,
        name="factor",
        out_shape=jax.ShapeDtypeStruct((4, WIDTH, LANES), F32),
        in_specs=[vmem()],
        out_specs=vmem(),
        scratch_shapes=[pltpu.VMEM((2 * LANES, LANES), F32)],
        compiler_params=PARAMS,
    )(gram)


def run_modes(slot, factor, s, weights, outputs=()):
    anywhere = pl.BlockSpec(memory_space=pl.ANY)
    return pl.pallas_call(
        functools.partial(modes_kernel, slot),
        name="modes_far" if slot else "modes_own",
        out_shape=(
            jax.ShapeDtypeStruct((2, SUBS, ROWS, LANES), BF16),
            jax.ShapeDtypeStruct((2, SUBS, WIDTH, WIDTH), F32),
        ),
        in_specs=[vmem()] * 3 + [anywhere] * len(outputs),
        out_specs=(anywhere, anywhere),
        scratch_shapes=[
            pltpu.VMEM((2, 2 * ROWS, LANES), F32),
            pltpu.VMEM((4, WIDTH, LANES), F32),
            pltpu.VMEM((2, 4, ROWS, LANES), BF16),
            pltpu.VMEM((2, 4, WIDTH, WIDTH), F32),
            pltpu.SemaphoreType.DMA((4,)),
            pltpu.SemaphoreType.DMA((4,)),
        ],
        input_output_aliases={3: 0, 4: 1} if outputs else {},
        compiler_params=PARAMS,
        cost_estimate=pl.CostEstimate(flops=3 * 10**8, bytes_accessed=2**22, transcendentals=0),
    )(factor, s, weights, *outputs)


def space_perm(along, shift):
    pairs = []
    for i in range(32):
        z, x, core = i // 8, i // 2 % 4, i % 2
        if along == "x":
            x = (x + shift) % 4
        elif along == "z":
            z = (z + shift) % 4
        else:
            core = 1 - core
        pairs.append((i, (z * 4 + x) * 2 + core))
    return pairs


def sum_over_chips(value):
    for along in ("x", "z"):
        far = [lax.ppermute(value, "space", space_perm(along, d)) for d in (3, 1, 2)]
        value = ((value + far[0]) + far[1]) + far[2]
    return value


def on_device(spectra, weights):
    t = lax.axis_index("tm")
    flat = spectra.reshape(2, 2, 4, ROWS, LANES)

    def piece(d, source):
        return lax.dynamic_index_in_dim(source, (t + d) % 4, 2, keepdims=False)

    def move(d, source):
        return lax.ppermute(piece(d, source), "tm", [(i, (i + d) % 4) for i in range(4)])

    near = {}
    first = piece(2, flat)
    later, first = lax.optimization_barrier((flat, first))
    near[2] = lax.ppermute(first, "tm", [(i, (i + 2) % 4) for i in range(4)])
    for d in (3, 1):
        near[d] = move(d, later)
    last, near[2] = lax.optimization_barrier((flat, near[2]))
    own = piece(0, last)
    even = run_even(own, near[2], weights)
    other, s_far, send = run_send(near[3], near[1], weights, even)
    across = space_perm("core", 1)
    arrived = lax.ppermute(send, "space", across)
    s_own, keep = run_keep(other)
    gram = sum_over_chips(keep + arrived)
    factor = run_factor(gram)
    far = lax.ppermute(factor, "space", across)
    outputs = run_modes(0, factor, s_own, weights)
    modes, upper = run_modes(1, far, s_far, weights, outputs)
    return (
        modes.reshape(2, SUBS, 1, WIDTH, FIELDS, LANES),
        upper.reshape(2, SUBS, 1, WIDTH, WIDTH),
    )


def solution(mesh):
    placed = (P(None, "tm", None, None, None, "space"), P(None, "space"))
    return jax.shard_map(
        on_device,
        mesh=mesh,
        in_specs=placed,
        out_specs=(P(None, None, "tm", None, None, "space"), P(None, None, "tm", None, None)),
        check_vma=False,
    )
```

```python
import functools
import math

import jax
import jax.numpy as jnp
import numpy as np
from jax import lax
from jax.experimental import pallas as pl
from jax.experimental.pallas import tpu as pltpu
from jax.sharding import PartitionSpec as P

SUBS = 8
WIDTH = 64
FIELDS = 4
LANES = 128
ROWS = WIDTH * FIELDS
F32 = jnp.float32
BF16 = jnp.bfloat16


def by_bin(t, values):
    values = [float(v) for v in values]
    if len(set(values)) == 1:
        return F32(values[0])
    return jnp.where(
        t < 2, jnp.where(t == 0, values[0], values[1]), jnp.where(t == 2, values[2], values[3])
    ).astype(F32)


def unit(t, angles):
    return by_bin(t, np.cos(angles)), by_bin(t, np.sin(angles))


def source_twiddle(t, d):
    return unit(t, [-2.0 * math.pi * (((b - d) % 4) * b) / 16.0 for b in range(4)])


def second_twiddle(t, q):
    return unit(t, [-2.0 * math.pi * (b / 32.0 + q / 8.0) for b in range(4)])


def split(value):
    high = value.astype(BF16)
    return high, (value - high.astype(F32)).astype(BF16)


def lane_iota(shape):
    return lax.broadcasted_iota(jnp.int32, shape, len(shape) - 1)


SMALL = (8, LANES)


def places():
    lane = lane_iota(SMALL)
    sub = lax.broadcasted_iota(jnp.int32, SMALL, 0)
    parity = lane // WIDTH
    group = lane % 16
    return lane, sub, parity, group, group * 4 + sub % 4


def block_transpose(tiles):
    block = lane_iota(tiles[0].shape) // 16
    for bit in range(3):
        step = 1 << bit
        low = (block & step) == 0
        out = list(tiles)
        for x in range(8):
            if x & step == 0:
                y = x | step
                out[x] = jnp.where(low, tiles[x], pltpu.roll(tiles[y], 16 * step, 1))
                out[y] = jnp.where(low, pltpu.roll(tiles[x], LANES - 16 * step, 1), tiles[y])
        tiles = out
    return tiles


def gather_lanes(value, index):
    return jnp.take_along_axis(value, index, axis=1)


def reverse_rows(value, lane, sub):
    index = (1 - lane // WIDTH) * WIDTH + (lane % WIDTH) // 16 * 16 + 15 - lane % 16
    value = gather_lanes(value, index)
    value = jnp.where(sub % 2 == 0, pltpu.roll(value, 7, 0), pltpu.roll(value, 1, 0))
    return jnp.where(sub % 4 < 2, pltpu.roll(value, 6, 0), pltpu.roll(value, 2, 0))


def pack_gram(work, s_ref, out_ref, mixed, products):
    left = lane_iota((WIDTH, LANES)) < WIDTH
    for q in range(4):
        for part in range(2):
            for f in range(FIELDS):
                for j in range(4):
                    value = work[q, part, pl.ds(j * 4 + f, 16, stride=16), :]
                    high, low = split(value)
                    row = part * WIDTH + j * 16
                    s_ref[q, row : row + 16, f * LANES : (f + 1) * LANES] = high
                    s_ref[q, LANES + row : LANES + row + 16, f * LANES : (f + 1) * LANES] = low

    for q in range(4):
        products[q] = lax.dot_general(
            s_ref[q], s_ref[q, :LANES], (((1,), (1,)), ((), ())), preferred_element_type=F32
        )

    tiles = [None] * 8
    for q in range(4):
        cross = products[q, LANES:]
        full = products[q, :LANES] + (cross + cross.T)
        low = pltpu.roll(full[WIDTH:], WIDTH, 1)
        tile = full[:WIDTH] + jnp.where(left, low, -low)
        for p in range(2):
            tiles[p * 4 + q] = jnp.concatenate(
                [tile[p * 16 : p * 16 + 16], tile[32 + p * 16 : 48 + p * 16]], axis=0
            )
    for a, tile in enumerate(block_transpose(tiles)):
        mixed[a * 32 : (a + 1) * 32, :] = tile
    lane, sub, parity, _, column = places()
    for m in range(16):
        near = mixed[pl.ds(m % 2 * 16 + m // 2, 8, stride=32), :]
        far_m = 31 - m
        far = mixed[pl.ds(far_m % 2 * 16 + far_m // 2, 8, stride=32), :]
        far = reverse_rows(far, lane, sub)
        line = 2 * m + parity
        far = jnp.where(column == line, pltpu.roll(far, 4, 0), far)
        upper = (column > line) | ((column == line) & (sub < 4))
        out_ref[m * 8 : (m + 1) * 8, :] = jnp.where(upper, near, far)


def twiddles(weight, shifts):
    t = lax.axis_index("tm")
    root = jnp.sqrt(jnp.concatenate([weight[...]] * 4, axis=0))
    out = []
    for d in shifts:
        re, im = source_twiddle(t, d)
        out.append((root * re, root * im))
    return out


def twisted(source, s, rows, tw):
    re = source[0, s, rows, :].astype(F32)
    im = source[1, s, rows, :].astype(F32)
    return re * tw[0] - im * tw[1], re * tw[1] + im * tw[0]


def even_kernel(own, near2, weight, even_ref):
    tw = twiddles(weight, (0, 2))

    def step(index, _):
        rows = pl.ds(pl.multiple_of(index * 16, 16), 16)
        for s in range(2):
            y0 = twisted(own, s, rows, tw[0])
            y2 = twisted(near2, s, rows, tw[1])
            even_ref[s, 0, rows, :] = y0[0] + y2[0]
            even_ref[s, 1, rows, :] = y0[1] + y2[1]
            even_ref[s, 2, rows, :] = y0[0] - y2[0]
            even_ref[s, 3, rows, :] = y0[1] - y2[1]
        return 0

    lax.fori_loop(0, ROWS // 16, step, 0, unroll=4)


def send_kernel(near3, near1, weight, even, other_ref, s_ref, send_ref, work, mixed, products):
    t = lax.axis_index("tm")
    side = jnp.where(lax.axis_index("space") % 2 == 0, -1.0, 1.0).astype(F32)
    tw = twiddles(weight, (1, 3))
    tq = []
    for q in range(4):
        re, im = second_twiddle(t, q)
        tq.append((re * side, im * side))

    def step(index, _):
        rows = pl.ds(pl.multiple_of(index * 16, 16), 16)
        radix = []
        for s in range(2):
            y1 = twisted(near1, s, rows, tw[0])
            y3 = twisted(near3, s, rows, tw[1])
            a = (even[s, 0, rows, :], even[s, 1, rows, :])
            b = (even[s, 2, rows, :], even[s, 3, rows, :])
            c = (y1[0] + y3[0], y1[1] + y3[1])
            e = (y1[0] - y3[0], y1[1] - y3[1])
            radix.append(
                [
                    (a[0] + c[0], a[1] + c[1]),
                    (b[0] - e[1], b[1] + e[0]),
                    (a[0] - c[0], a[1] - c[1]),
                    (b[0] + e[1], b[1] - e[0]),
                ]
            )
        for q in range(4):
            x0 = radix[0][q]
            x1 = radix[1][q]
            v = (x1[0] * tq[q][0] - x1[1] * tq[q][1], x1[0] * tq[q][1] + x1[1] * tq[q][0])
            work[q, 0, rows, :] = x0[0] + v[0]
            work[q, 1, rows, :] = x0[1] + v[1]
            other_ref[q, 0, rows, :] = x0[0] - v[0]
            other_ref[q, 1, rows, :] = x0[1] - v[1]
        return 0

    lax.fori_loop(0, ROWS // 16, step, 0, unroll=4)
    pack_gram(work, s_ref, send_ref, mixed, products)


def at_sub(value, index):
    return jnp.broadcast_to(value[index : index + 1, :], value.shape)


def factor_kernel(gram, out_ref, spread):
    lane, sub, parity, group, column = places()
    first = parity == 0
    sign = jnp.where(sub < 4, 1.0, -1.0).astype(F32)
    real = sub < 4
    lane_base = lane // 16 * 16

    def turn(value):
        return pltpu.roll(value, 4, 0) * sign

    def lifted(value):
        return jnp.where(first, value, pltpu.roll(value, 7, 0))

    rows = [None] * 32
    for m in range(16):
        packed = gram[m * 8 : (m + 1) * 8, :]
        rows[m] = packed
        far = reverse_rows(packed, lane, sub)
        line = 2 * (31 - m) + parity
        rows[31 - m] = jnp.where(column == line, pltpu.roll(far, 4, 0), far)

    def block_of(v, p, g):
        return gather_lanes(v, lane % WIDTH // 16 * 16 + p * WIDTH + g)

    block = [block_of(rows[r // 2], r % 2, 0) for r in range(4)]
    for g in range(16):
        last = g == 15
        full, ahead, following = [], [], []
        for v in (rows[2 * g], rows[2 * g + 1]):
            turned = pltpu.roll(v, WIDTH, 1)
            full += [jnp.where(first, v, turned), jnp.where(first, turned, v)]
        if not last:
            ahead = [block_of(rows[2 * g + r // 2], r % 2, g + 1) for r in range(4)]
            following = [block_of(rows[2 * g + 2 + r // 2], r % 2, g + 1) for r in range(4)]
        in_group = group == g
        root, scaled = [], []
        for s in range(4):
            here = in_group & (sub % 4 == s)
            pivot = at_sub(block[s], s)
            ip = 1.0 / pivot
            root.append(lax.rsqrt(pivot))
            full[s] = jnp.where(here, jnp.where(real, 1.0, 0.0), full[s])
            y = full[s] * ip
            y_t = turn(y)
            b = block[s] * ip
            b_t = turn(b)
            if not last:
                n = ahead[s] * ip
                n_t = turn(n)
                for r in range(4):
                    mr = at_sub(ahead[s], r)
                    mi = at_sub(ahead[s], 4 + r)
                    following[r] = following[r] - (mr * n + mi * n_t)
            for r in range(s + 1, 4):
                mr = at_sub(block[s], r)
                mi = at_sub(block[s], 4 + r)
                full[r] = jnp.where(here, 0.0, full[r]) - (mr * y + mi * y_t)
                block[r] = block[r] - (mr * b + mi * b_t)
                if not last:
                    ahead[r] = ahead[r] - (mr * n + mi * n_t)
            later = in_group & (sub % 4 > s)
            scaled.append((jnp.where(later, 0.0, y), jnp.where(later, 0.0, y_t)))
        raised = [lifted(full[r]) for r in range(4)]
        for h in range(g + 1, 16):
            if h == g + 1:
                multi = [lifted(ahead[r]) for r in range(4)]
            else:
                multi = [gather_lanes(raised[r], lane_base + h) for r in range(4)]
            for odd in range(2):
                m = 2 * h + odd
                value = jnp.where(in_group, 0.0, rows[m])
                terms = []
                for r in range(4):
                    y, y_t = scaled[r]
                    terms.append(at_sub(multi[r], 2 * odd) * y + at_sub(multi[r], 4 + 2 * odd) * y_t)
                rows[m] = value - ((terms[0] + terms[1]) + (terms[2] + terms[3]))
        block = following
        for odd in range(2):
            m = 2 * g + odd
            spread[m * 8 : (m + 1) * 8, :] = jnp.where(
                first, full[2 * odd] * root[2 * odd], full[2 * odd + 1] * root[2 * odd + 1]
            )
        if g % 4 == 3:
            k = g // 4
            tiles = [spread[pl.ds(k * WIDTH + a, 8, stride=8), :] for a in range(8)]
            for b, tile in enumerate(block_transpose(tiles)):
                row = b // 4 * 32 + k * 8
                out_ref[b % 4, row : row + 8, :] = tile


def modes_kernel(slot, *refs):
    if slot == 0:
        source, s_ref, weight = refs[:3]
    else:
        source, s_ref, weight, _, _ = refs[:5]
    modes_ref, upper_ref, work, natural, modes_own, upper_own, modes_sem, upper_sem = refs[-8:]
    t = lax.axis_index("tm")
    mine = (lax.axis_index("space") + slot) % 2
    wide = (WIDTH, LANES)
    lane = lane_iota(wide)
    order = lax.broadcasted_iota(jnp.int32, wide, 0)
    line = order % 32 * 2 + order // 32
    column = lane % 16 * 4 + lane // 16 % 4
    left = lane < WIDTH
    lane8 = lane_iota(SMALL)
    natural_index = lane8 // WIDTH * WIDTH + lane8 % 4 * 16 + lane8 % WIDTH // 4
    root = lax.rsqrt(weight[...])

    copies = []
    for k in range(4):
        q = mine * 4 + k
        both = source[k]
        inverse = jnp.where(column <= line, both, 0.0)
        diag = jnp.where(left, 1.0 / both, 0.0)
        upper = jnp.where(column > line, both, jnp.where(column == line, diag, 0.0))
        for j in range(8):
            piece = gather_lanes(upper[j * 8 : j * 8 + 8], natural_index)
            natural[k, pl.ds(j // 4 + j % 4 * 16, 8, stride=2), :] = piece
        upper_own[0, k] = natural[k, :, :WIDTH]
        upper_own[1, k] = natural[k, :, WIDTH:]
        copies.append(
            pltpu.make_async_copy(upper_own.at[:, k], upper_ref.at[:, q], upper_sem.at[k])
        )
        copies[-1].start()
        swapped = pltpu.roll(inverse, WIDTH, 1)
        swapped = jnp.where(left, -swapped, swapped)
        pr = by_bin(t, [(1, 0, -1, 0)[b * k % 4] for b in range(4)])
        pi = by_bin(t, [(0, -1, 0, 1)[b * k % 4] for b in range(4)])
        lhs = jnp.concatenate([pr * inverse - pi * swapped, pr * swapped + pi * inverse], axis=0)
        lh, ll = split(lhs)
        out = jnp.dot(jnp.concatenate([lh, lh], axis=1), s_ref[k], preferred_element_type=F32)
        out = out + jnp.dot(ll, s_ref[k, :LANES], preferred_element_type=F32)
        for part in range(2):
            for f in range(FIELDS):
                for p in range(2):
                    row = part * WIDTH + p * 32
                    block = out[row : row + 32, f * LANES : (f + 1) * LANES] * root[f : f + 1, :]
                    work[k % 2, pl.ds(part * ROWS + p * 4 + f, 32, stride=8), :] = block
            modes_own[part, k] = work[k % 2, part * ROWS : (part + 1) * ROWS, :].astype(BF16)
        copies.append(
            pltpu.make_async_copy(modes_own.at[:, k], modes_ref.at[:, q], modes_sem.at[k])
        )
        copies[-1].start()
    for copy in copies:
        copy.wait()


def vmem():
    return pl.BlockSpec(memory_space=pltpu.VMEM)


HALF = (LANES, LANES)
PARAMS = pltpu.CompilerParams(vmem_limit_bytes=32 * 1024 * 1024)


def run_even(own, near2, weights):
    return pl.pallas_call(
        even_kernel,
        name="even",
        out_shape=jax.ShapeDtypeStruct((2, 4, ROWS, LANES), F32),
        in_specs=[vmem()] * 3,
        out_specs=vmem(),
        compiler_params=PARAMS,
        cost_estimate=pl.CostEstimate(flops=2**22, bytes_accessed=2**21, transcendentals=0),
    )(own, near2, weights)


def run_send(near3, near1, weights, even):
    return pl.pallas_call(
        send_kernel,
        name="send_gram",
        out_shape=(
            jax.ShapeDtypeStruct((4, 2, ROWS, LANES), F32),
            jax.ShapeDtypeStruct((4, 2 * LANES, FIELDS * LANES), BF16),
            jax.ShapeDtypeStruct(HALF, F32),
        ),
        in_specs=[vmem()] * 4,
        out_specs=(vmem(),) * 3,
        scratch_shapes=[
            pltpu.VMEM((4, 2, ROWS, LANES), F32),
            pltpu.VMEM((ROWS, LANES), F32),
            pltpu.VMEM((4, 2 * LANES, LANES), F32),
        ],
        compiler_params=PARAMS,
    )(near3, near1, weights, even)


def run_keep(work):
    return pl.pallas_call(
        pack_gram,
        name="keep_gram",
        out_shape=(
            jax.ShapeDtypeStruct((4, 2 * LANES, FIELDS * LANES), BF16),
            jax.ShapeDtypeStruct(HALF, F32),
        ),
        in_specs=[vmem()],
        out_specs=(vmem(),) * 2,
        scratch_shapes=[
            pltpu.VMEM((ROWS, LANES), F32),
            pltpu.VMEM((4, 2 * LANES, LANES), F32),
        ],
        compiler_params=PARAMS,
        cost_estimate=pl.CostEstimate(flops=3 * 10**8, bytes_accessed=2**21, transcendentals=0),
    )(work)


def run_factor(gram):
    return pl.pallas_call(
        factor_kernel,
        name="factor",
        out_shape=jax.ShapeDtypeStruct((4, WIDTH, LANES), F32),
        in_specs=[vmem()],
        out_specs=vmem(),
        scratch_shapes=[pltpu.VMEM((2 * LANES, LANES), F32)],
        compiler_params=PARAMS,
    )(gram)


def run_modes(slot, factor, s, weights, outputs=()):
    anywhere = pl.BlockSpec(memory_space=pl.ANY)
    return pl.pallas_call(
        functools.partial(modes_kernel, slot),
        name="modes_far" if slot else "modes_own",
        out_shape=(
            jax.ShapeDtypeStruct((2, SUBS, ROWS, LANES), BF16),
            jax.ShapeDtypeStruct((2, SUBS, WIDTH, WIDTH), F32),
        ),
        in_specs=[vmem()] * 3 + [anywhere] * len(outputs),
        out_specs=(anywhere, anywhere),
        scratch_shapes=[
            pltpu.VMEM((2, 2 * ROWS, LANES), F32),
            pltpu.VMEM((4, WIDTH, LANES), F32),
            pltpu.VMEM((2, 4, ROWS, LANES), BF16),
            pltpu.VMEM((2, 4, WIDTH, WIDTH), F32),
            pltpu.SemaphoreType.DMA((4,)),
            pltpu.SemaphoreType.DMA((4,)),
        ],
        input_output_aliases={3: 0, 4: 1} if outputs else {},
        compiler_params=PARAMS,
        cost_estimate=pl.CostEstimate(flops=3 * 10**8, bytes_accessed=2**22, transcendentals=0),
    )(factor, s, weights, *outputs)


def space_perm(first, shift):
    pairs = []
    for i in range(32):
        z, x, core = i // 8, i // 2 % 4, i % 2
        if shift == 0:
            core = 1 - core
        elif first == (core == 0):
            x = (x + shift) % 4
        else:
            z = (z + shift) % 4
        pairs.append((i, (z * 4 + x) * 2 + core))
    return pairs


def sum_over_chips(value):
    for first in (True, False):
        far = [lax.ppermute(value, "space", space_perm(first, d)) for d in (3, 1, 2)]
        value = ((value + far[0]) + far[1]) + far[2]
    return value


def on_device(spectra, weights):
    t = lax.axis_index("tm")
    flat = spectra.reshape(2, 2, 4, ROWS, LANES)

    def piece(d, source):
        return lax.dynamic_index_in_dim(source, (t + d) % 4, 2, keepdims=False)

    def move(d, source):
        return lax.ppermute(piece(d, source), "tm", [(i, (i + d) % 4) for i in range(4)])

    near = {}
    first = piece(2, flat)
    later, first = lax.optimization_barrier((flat, first))
    near[2] = lax.ppermute(first, "tm", [(i, (i + 2) % 4) for i in range(4)])
    for d in (3, 1):
        near[d] = move(d, later)
    last, near[2] = lax.optimization_barrier((flat, near[2]))
    own = piece(0, last)
    even = run_even(own, near[2], weights)
    other, s_far, send = run_send(near[3], near[1], weights, even)
    across = space_perm(True, 0)
    arrived = lax.ppermute(send, "space", across)
    s_own, keep = run_keep(other)
    gram = sum_over_chips(keep + arrived)
    factor = run_factor(gram)
    far = lax.ppermute(factor, "space", across)
    outputs = run_modes(0, factor, s_own, weights)
    modes, upper = run_modes(1, far, s_far, weights, outputs)
    return (
        modes.reshape(2, SUBS, 1, WIDTH, FIELDS, LANES),
        upper.reshape(2, SUBS, 1, WIDTH, WIDTH),
    )


def solution(mesh):
    placed = (P(None, "tm", None, None, None, "space"), P(None, "space"))
    return jax.shard_map(
        on_device,
        mesh=mesh,
        in_specs=placed,
        out_specs=(P(None, None, "tm", None, None, "space"), P(None, None, "tm", None, None)),
        check_vma=False,
    )
```

```python
import functools
import math

import jax
import jax.numpy as jnp
import numpy as np
from jax import lax
from jax.experimental import pallas as pl
from jax.experimental.pallas import tpu as pltpu
from jax.sharding import PartitionSpec as P

SUBS = 8
WIDTH = 64
FIELDS = 4
LANES = 128
ROWS = WIDTH * FIELDS
F32 = jnp.float32
BF16 = jnp.bfloat16


def by_bin(t, values):
    values = [float(v) for v in values]
    if len(set(values)) == 1:
        return F32(values[0])
    return jnp.where(
        t < 2, jnp.where(t == 0, values[0], values[1]), jnp.where(t == 2, values[2], values[3])
    ).astype(F32)


def unit(t, angles):
    return by_bin(t, np.cos(angles)), by_bin(t, np.sin(angles))


def source_twiddle(t, d):
    return unit(t, [-2.0 * math.pi * (((b - d) % 4) * b) / 16.0 for b in range(4)])


def second_twiddle(t, q):
    return unit(t, [-2.0 * math.pi * (b / 32.0 + q / 8.0) for b in range(4)])


def split(value):
    high = value.astype(BF16)
    return high, (value - high.astype(F32)).astype(BF16)


def lane_iota(shape):
    return lax.broadcasted_iota(jnp.int32, shape, len(shape) - 1)


SMALL = (8, LANES)


def places():
    lane = lane_iota(SMALL)
    sub = lax.broadcasted_iota(jnp.int32, SMALL, 0)
    parity = lane // WIDTH
    group = lane % 16
    return lane, sub, parity, group, group * 4 + sub % 4


def block_transpose(tiles):
    block = lane_iota(tiles[0].shape) // 16
    for bit in range(3):
        step = 1 << bit
        low = (block & step) == 0
        out = list(tiles)
        for x in range(8):
            if x & step == 0:
                y = x | step
                out[x] = jnp.where(low, tiles[x], pltpu.roll(tiles[y], 16 * step, 1))
                out[y] = jnp.where(low, pltpu.roll(tiles[x], LANES - 16 * step, 1), tiles[y])
        tiles = out
    return tiles


def gather_lanes(value, index):
    return jnp.take_along_axis(value, index, axis=1)


def reverse_rows(value, lane, sub):
    index = (1 - lane // WIDTH) * WIDTH + (lane % WIDTH) // 16 * 16 + 15 - lane % 16
    value = gather_lanes(value, index)
    value = jnp.where(sub % 2 == 0, pltpu.roll(value, 7, 0), pltpu.roll(value, 1, 0))
    return jnp.where(sub % 4 < 2, pltpu.roll(value, 6, 0), pltpu.roll(value, 2, 0))


def pack_gram(work, s_ref, out_ref, mixed, products):
    left = lane_iota((WIDTH, LANES)) < WIDTH
    for q in range(4):
        for part in range(2):
            for f in range(FIELDS):
                for j in range(4):
                    value = work[q, part, pl.ds(j * 4 + f, 16, stride=16), :]
                    high, low = split(value)
                    row = part * WIDTH + j * 16
                    s_ref[q, row : row + 16, f * LANES : (f + 1) * LANES] = high
                    s_ref[q, LANES + row : LANES + row + 16, f * LANES : (f + 1) * LANES] = low

    for q in range(4):
        products[q] = lax.dot_general(
            s_ref[q], s_ref[q, :LANES], (((1,), (1,)), ((), ())), preferred_element_type=F32
        )

    tiles = [None] * 8
    for q in range(4):
        cross = products[q, LANES:]
        full = products[q, :LANES] + (cross + cross.T)
        low = pltpu.roll(full[WIDTH:], WIDTH, 1)
        tile = full[:WIDTH] + jnp.where(left, low, -low)
        for p in range(2):
            tiles[p * 4 + q] = jnp.concatenate(
                [tile[p * 16 : p * 16 + 16], tile[32 + p * 16 : 48 + p * 16]], axis=0
            )
    for a, tile in enumerate(block_transpose(tiles)):
        mixed[a * 32 : (a + 1) * 32, :] = tile
    lane, sub, parity, _, column = places()
    for m in range(16):
        near = mixed[pl.ds(m % 2 * 16 + m // 2, 8, stride=32), :]
        far_m = 31 - m
        far = mixed[pl.ds(far_m % 2 * 16 + far_m // 2, 8, stride=32), :]
        far = reverse_rows(far, lane, sub)
        line = 2 * m + parity
        far = jnp.where(column == line, pltpu.roll(far, 4, 0), far)
        upper = (column > line) | ((column == line) & (sub < 4))
        out_ref[m * 8 : (m + 1) * 8, :] = jnp.where(upper, near, far)


def twiddles(weight, shifts):
    t = lax.axis_index("tm")
    root = jnp.sqrt(jnp.concatenate([weight[...]] * 4, axis=0))
    out = []
    for d in shifts:
        re, im = source_twiddle(t, d)
        out.append((root * re, root * im))
    return out


def twisted(source, s, rows, tw):
    re = source[0, s, rows, :].astype(F32)
    im = source[1, s, rows, :].astype(F32)
    return re * tw[0] - im * tw[1], re * tw[1] + im * tw[0]


def even_kernel(own, near2, weight, even_ref):
    tw = twiddles(weight, (0, 2))

    def step(index, _):
        rows = pl.ds(pl.multiple_of(index * 16, 16), 16)
        for s in range(2):
            y0 = twisted(own, s, rows, tw[0])
            y2 = twisted(near2, s, rows, tw[1])
            even_ref[s, 0, rows, :] = y0[0] + y2[0]
            even_ref[s, 1, rows, :] = y0[1] + y2[1]
            even_ref[s, 2, rows, :] = y0[0] - y2[0]
            even_ref[s, 3, rows, :] = y0[1] - y2[1]
        return 0

    lax.fori_loop(0, ROWS // 16, step, 0, unroll=4)


def send_kernel(near3, near1, weight, even, other_ref, s_ref, send_ref, work, mixed, products):
    t = lax.axis_index("tm")
    side = jnp.where(lax.axis_index("space") % 2 == 0, -1.0, 1.0).astype(F32)
    tw = twiddles(weight, (1, 3))
    tq = []
    for q in range(4):
        re, im = second_twiddle(t, q)
        tq.append((re * side, im * side))

    def step(index, _):
        rows = pl.ds(pl.multiple_of(index * 16, 16), 16)
        radix = []
        for s in range(2):
            y1 = twisted(near1, s, rows, tw[0])
            y3 = twisted(near3, s, rows, tw[1])
            a = (even[s, 0, rows, :], even[s, 1, rows, :])
            b = (even[s, 2, rows, :], even[s, 3, rows, :])
            c = (y1[0] + y3[0], y1[1] + y3[1])
            e = (y1[0] - y3[0], y1[1] - y3[1])
            radix.append(
                [
                    (a[0] + c[0], a[1] + c[1]),
                    (b[0] - e[1], b[1] + e[0]),
                    (a[0] - c[0], a[1] - c[1]),
                    (b[0] + e[1], b[1] - e[0]),
                ]
            )
        for q in range(4):
            x0 = radix[0][q]
            x1 = radix[1][q]
            v = (x1[0] * tq[q][0] - x1[1] * tq[q][1], x1[0] * tq[q][1] + x1[1] * tq[q][0])
            work[q, 0, rows, :] = x0[0] + v[0]
            work[q, 1, rows, :] = x0[1] + v[1]
            other_ref[q, 0, rows, :] = x0[0] - v[0]
            other_ref[q, 1, rows, :] = x0[1] - v[1]
        return 0

    lax.fori_loop(0, ROWS // 16, step, 0, unroll=4)
    pack_gram(work, s_ref, send_ref, mixed, products)


def at_sub(value, index):
    return jnp.broadcast_to(value[index : index + 1, :], value.shape)


def factor_kernel(gram, out_ref, spread):
    lane, sub, parity, group, column = places()
    first = parity == 0
    sign = jnp.where(sub < 4, 1.0, -1.0).astype(F32)
    real = sub < 4
    lane_base = lane // 16 * 16

    def turn(value):
        return pltpu.roll(value, 4, 0) * sign

    def lifted(value):
        return jnp.where(first, value, pltpu.roll(value, 7, 0))

    rows = [None] * 32
    for m in range(16):
        packed = gram[m * 8 : (m + 1) * 8, :]
        rows[m] = packed
        far = reverse_rows(packed, lane, sub)
        line = 2 * (31 - m) + parity
        rows[31 - m] = jnp.where(column == line, pltpu.roll(far, 4, 0), far)

    def block_of(v, p, g):
        return gather_lanes(v, lane % WIDTH // 16 * 16 + p * WIDTH + g)

    block = [block_of(rows[r // 2], r % 2, 0) for r in range(4)]
    for g in range(16):
        last = g == 15
        full, ahead, following = [], [], []
        for v in (rows[2 * g], rows[2 * g + 1]):
            turned = pltpu.roll(v, WIDTH, 1)
            full += [jnp.where(first, v, turned), jnp.where(first, turned, v)]
        if not last:
            ahead = [block_of(rows[2 * g + r // 2], r % 2, g + 1) for r in range(4)]
            following = [block_of(rows[2 * g + 2 + r // 2], r % 2, g + 1) for r in range(4)]
        in_group = group == g
        root, scaled = [], []
        for s in range(4):
            here = in_group & (sub % 4 == s)
            pivot = at_sub(block[s], s)
            ip = 1.0 / pivot
            root.append(lax.rsqrt(pivot))
            full[s] = jnp.where(here, jnp.where(real, 1.0, 0.0), full[s])
            y = full[s] * ip
            y_t = turn(y)
            b = block[s] * ip
            b_t = turn(b)
            if not last:
                n = ahead[s] * ip
                n_t = turn(n)
                for r in range(4):
                    mr = at_sub(ahead[s], r)
                    mi = at_sub(ahead[s], 4 + r)
                    following[r] = following[r] - (mr * n + mi * n_t)
            for r in range(s + 1, 4):
                mr = at_sub(block[s], r)
                mi = at_sub(block[s], 4 + r)
                full[r] = jnp.where(here, 0.0, full[r]) - (mr * y + mi * y_t)
                block[r] = block[r] - (mr * b + mi * b_t)
                if not last:
                    ahead[r] = ahead[r] - (mr * n + mi * n_t)
            later = in_group & (sub % 4 > s)
            scaled.append((jnp.where(later, 0.0, y), jnp.where(later, 0.0, y_t)))
        raised = [lifted(full[r]) for r in range(4)]
        for h in range(g + 1, 16):
            if h == g + 1:
                multi = [lifted(ahead[r]) for r in range(4)]
            else:
                multi = [gather_lanes(raised[r], lane_base + h) for r in range(4)]
            for odd in range(2):
                m = 2 * h + odd
                value = jnp.where(in_group, 0.0, rows[m])
                terms = []
                for r in range(4):
                    y, y_t = scaled[r]
                    terms.append(at_sub(multi[r], 2 * odd) * y + at_sub(multi[r], 4 + 2 * odd) * y_t)
                rows[m] = value - ((terms[0] + terms[1]) + (terms[2] + terms[3]))
        block = following
        for odd in range(2):
            m = 2 * g + odd
            spread[m * 8 : (m + 1) * 8, :] = jnp.where(
                first, full[2 * odd] * root[2 * odd], full[2 * odd + 1] * root[2 * odd + 1]
            )
        if g % 4 == 3:
            k = g // 4
            tiles = [spread[pl.ds(k * WIDTH + a, 8, stride=8), :] for a in range(8)]
            for b, tile in enumerate(block_transpose(tiles)):
                row = b // 4 * 32 + k * 8
                out_ref[b % 4, row : row + 8, :] = tile


def modes_kernel(slot, *refs):
    if slot == 0:
        source, s_ref, weight = refs[:3]
    else:
        source, s_ref, weight, _, _ = refs[:5]
    modes_ref, upper_ref, work, natural, modes_own, upper_own, modes_sem, upper_sem = refs[-8:]
    t = lax.axis_index("tm")
    mine = (lax.axis_index("space") + slot) % 2
    wide = (WIDTH, LANES)
    lane = lane_iota(wide)
    order = lax.broadcasted_iota(jnp.int32, wide, 0)
    line = order % 32 * 2 + order // 32
    column = lane % 16 * 4 + lane // 16 % 4
    left = lane < WIDTH
    lane8 = lane_iota(SMALL)
    natural_index = lane8 // WIDTH * WIDTH + lane8 % 4 * 16 + lane8 % WIDTH // 4
    root = lax.rsqrt(weight[...])

    copies = []
    for k in range(4):
        q = mine * 4 + k
        both = source[k]
        inverse = jnp.where(column <= line, both, 0.0)
        diag = jnp.where(left, 1.0 / both, 0.0)
        upper = jnp.where(column > line, both, jnp.where(column == line, diag, 0.0))
        for j in range(8):
            piece = gather_lanes(upper[j * 8 : j * 8 + 8], natural_index)
            natural[k, pl.ds(j // 4 + j % 4 * 16, 8, stride=2), :] = piece
        upper_own[0, k] = natural[k, :, :WIDTH]
        upper_own[1, k] = natural[k, :, WIDTH:]
        copies.append(
            pltpu.make_async_copy(upper_own.at[:, k], upper_ref.at[:, q], upper_sem.at[k])
        )
        copies[-1].start()
        swapped = pltpu.roll(inverse, WIDTH, 1)
        swapped = jnp.where(left, -swapped, swapped)
        pr = by_bin(t, [(1, 0, -1, 0)[b * k % 4] for b in range(4)])
        pi = by_bin(t, [(0, -1, 0, 1)[b * k % 4] for b in range(4)])
        lhs = jnp.concatenate([pr * inverse - pi * swapped, pr * swapped + pi * inverse], axis=0)
        lh, ll = split(lhs)
        out = jnp.dot(jnp.concatenate([lh, lh], axis=1), s_ref[k], preferred_element_type=F32)
        out = out + jnp.dot(ll, s_ref[k, :LANES], preferred_element_type=F32)
        for part in range(2):
            for f in range(FIELDS):
                for p in range(2):
                    row = part * WIDTH + p * 32
                    block = out[row : row + 32, f * LANES : (f + 1) * LANES] * root[f : f + 1, :]
                    work[k % 2, pl.ds(part * ROWS + p * 4 + f, 32, stride=8), :] = block
            modes_own[part, k] = work[k % 2, part * ROWS : (part + 1) * ROWS, :].astype(BF16)
        copies.append(
            pltpu.make_async_copy(modes_own.at[:, k], modes_ref.at[:, q], modes_sem.at[k])
        )
        copies[-1].start()
    for copy in copies:
        copy.wait()


def vmem():
    return pl.BlockSpec(memory_space=pltpu.VMEM)


HALF = (LANES, LANES)
PARAMS = pltpu.CompilerParams(vmem_limit_bytes=32 * 1024 * 1024)


def run_even(own, near2, weights):
    return pl.pallas_call(
        even_kernel,
        name="even",
        out_shape=jax.ShapeDtypeStruct((2, 4, ROWS, LANES), F32),
        in_specs=[vmem()] * 3,
        out_specs=vmem(),
        compiler_params=PARAMS,
        cost_estimate=pl.CostEstimate(flops=2**22, bytes_accessed=2**21, transcendentals=0),
    )(own, near2, weights)


def run_send(near3, near1, weights, even):
    return pl.pallas_call(
        send_kernel,
        name="send_gram",
        out_shape=(
            jax.ShapeDtypeStruct((4, 2, ROWS, LANES), F32),
            jax.ShapeDtypeStruct((4, 2 * LANES, FIELDS * LANES), BF16),
            jax.ShapeDtypeStruct(HALF, F32),
        ),
        in_specs=[vmem()] * 4,
        out_specs=(vmem(),) * 3,
        scratch_shapes=[
            pltpu.VMEM((4, 2, ROWS, LANES), F32),
            pltpu.VMEM((ROWS, LANES), F32),
            pltpu.VMEM((4, 2 * LANES, LANES), F32),
        ],
        compiler_params=PARAMS,
    )(near3, near1, weights, even)


def run_keep(work):
    return pl.pallas_call(
        pack_gram,
        name="keep_gram",
        out_shape=(
            jax.ShapeDtypeStruct((4, 2 * LANES, FIELDS * LANES), BF16),
            jax.ShapeDtypeStruct(HALF, F32),
        ),
        in_specs=[vmem()],
        out_specs=(vmem(),) * 2,
        scratch_shapes=[
            pltpu.VMEM((ROWS, LANES), F32),
            pltpu.VMEM((4, 2 * LANES, LANES), F32),
        ],
        compiler_params=PARAMS,
        cost_estimate=pl.CostEstimate(flops=3 * 10**8, bytes_accessed=2**21, transcendentals=0),
    )(work)


def run_factor(gram):
    return pl.pallas_call(
        factor_kernel,
        name="factor",
        out_shape=jax.ShapeDtypeStruct((4, WIDTH, LANES), F32),
        in_specs=[vmem()],
        out_specs=vmem(),
        scratch_shapes=[pltpu.VMEM((2 * LANES, LANES), F32)],
        compiler_params=PARAMS,
    )(gram)


def run_modes(slot, factor, s, weights, outputs=()):
    anywhere = pl.BlockSpec(memory_space=pl.ANY)
    return pl.pallas_call(
        functools.partial(modes_kernel, slot),
        name="modes_far" if slot else "modes_own",
        out_shape=(
            jax.ShapeDtypeStruct((2, SUBS, ROWS, LANES), BF16),
            jax.ShapeDtypeStruct((2, SUBS, WIDTH, WIDTH), F32),
        ),
        in_specs=[vmem()] * 3 + [anywhere] * len(outputs),
        out_specs=(anywhere, anywhere),
        scratch_shapes=[
            pltpu.VMEM((2, 2 * ROWS, LANES), F32),
            pltpu.VMEM((4, WIDTH, LANES), F32),
            pltpu.VMEM((2, 4, ROWS, LANES), BF16),
            pltpu.VMEM((2, 4, WIDTH, WIDTH), F32),
            pltpu.SemaphoreType.DMA((4,)),
            pltpu.SemaphoreType.DMA((4,)),
        ],
        input_output_aliases={3: 0, 4: 1} if outputs else {},
        compiler_params=PARAMS,
        cost_estimate=pl.CostEstimate(flops=3 * 10**8, bytes_accessed=2**22, transcendentals=0),
    )(factor, s, weights, *outputs)


def space_perm(along, shift):
    pairs = []
    for i in range(32):
        z, x, core = i // 8, i // 2 % 4, i % 2
        if along == "x":
            x = (x + shift) % 4
        elif along == "z":
            z = (z + shift) % 4
        else:
            core = 1 - core
        pairs.append((i, (z * 4 + x) * 2 + core))
    return pairs


def sum_over_chips(value):
    for along in ("x", "z"):
        far = [lax.ppermute(value, "space", space_perm(along, d)) for d in (3, 1, 2)]
        value = ((value + far[0]) + far[1]) + far[2]
    return value


def on_device(spectra, weights):
    t = lax.axis_index("tm")
    flat = spectra.reshape(2, 2, 4, ROWS, LANES)

    def piece(d, source):
        return lax.dynamic_index_in_dim(source, (t + d) % 4, 2, keepdims=False)

    def move(d, source):
        return lax.ppermute(piece(d, source), "tm", [(i, (i + d) % 4) for i in range(4)])

    near = {}
    first = piece(2, flat)
    later, first = lax.optimization_barrier((flat, first))
    near[2] = lax.ppermute(first, "tm", [(i, (i + 2) % 4) for i in range(4)])
    for d in (3, 1):
        near[d] = move(d, later)
    last, near[2] = lax.optimization_barrier((flat, near[2]))
    own = piece(0, last)
    even = run_even(own, near[2], weights)
    other, s_far, send = run_send(near[3], near[1], weights, even)
    across = space_perm("core", 1)
    arrived = lax.ppermute(send, "space", across)
    s_own, keep = run_keep(other)
    gram = sum_over_chips(keep + arrived)
    factor = run_factor(gram)
    far = lax.ppermute(factor, "space", across)
    outputs = run_modes(0, factor, s_own, weights)
    modes, upper = run_modes(1, far, s_far, weights, outputs)
    return (
        modes.reshape(2, SUBS, 1, WIDTH, FIELDS, LANES),
        upper.reshape(2, SUBS, 1, WIDTH, WIDTH),
    )


def solution(mesh):
    placed = (P(None, "tm", None, None, None, "space"), P(None, "space"))
    return jax.shard_map(
        on_device,
        mesh=mesh,
        in_specs=placed,
        out_specs=(P(None, None, "tm", None, None, "space"), P(None, None, "tm", None, None)),
        check_vma=False,
    )
```

```python
import functools
import math

import jax
import jax.numpy as jnp
import numpy as np
from jax import lax
from jax.experimental import pallas as pl
from jax.experimental.pallas import tpu as pltpu
from jax.sharding import PartitionSpec as P

SUBS = 8
WIDTH = 64
FIELDS = 4
LANES = 128
ROWS = WIDTH * FIELDS
F32 = jnp.float32
BF16 = jnp.bfloat16


def by_bin(t, values):
    values = [float(v) for v in values]
    if len(set(values)) == 1:
        return F32(values[0])
    return jnp.where(
        t < 2, jnp.where(t == 0, values[0], values[1]), jnp.where(t == 2, values[2], values[3])
    ).astype(F32)


def unit(t, angles):
    return by_bin(t, np.cos(angles)), by_bin(t, np.sin(angles))


def source_twiddle(t, d):
    return unit(t, [-2.0 * math.pi * (((b - d) % 4) * b) / 16.0 for b in range(4)])


def second_twiddle(t, q):
    return unit(t, [-2.0 * math.pi * (b / 32.0 + q / 8.0) for b in range(4)])


def split(value):
    high = value.astype(BF16)
    return high, (value - high.astype(F32)).astype(BF16)


def lane_iota(shape):
    return lax.broadcasted_iota(jnp.int32, shape, len(shape) - 1)


SMALL = (8, LANES)


def places():
    lane = lane_iota(SMALL)
    sub = lax.broadcasted_iota(jnp.int32, SMALL, 0)
    parity = lane // WIDTH
    group = lane % 16
    return lane, sub, parity, group, group * 4 + sub % 4


def block_transpose(tiles):
    block = lane_iota(tiles[0].shape) // 16
    for bit in range(3):
        step = 1 << bit
        low = (block & step) == 0
        out = list(tiles)
        for x in range(8):
            if x & step == 0:
                y = x | step
                out[x] = jnp.where(low, tiles[x], pltpu.roll(tiles[y], 16 * step, 1))
                out[y] = jnp.where(low, pltpu.roll(tiles[x], LANES - 16 * step, 1), tiles[y])
        tiles = out
    return tiles


def gather_lanes(value, index):
    return jnp.take_along_axis(value, index, axis=1)


def reverse_rows(value, lane, sub):
    index = (1 - lane // WIDTH) * WIDTH + (lane % WIDTH) // 16 * 16 + 15 - lane % 16
    value = gather_lanes(value, index)
    value = jnp.where(sub % 2 == 0, pltpu.roll(value, 7, 0), pltpu.roll(value, 1, 0))
    return jnp.where(sub % 4 < 2, pltpu.roll(value, 6, 0), pltpu.roll(value, 2, 0))


def pack_gram(work, s_ref, out_ref, mixed, products):
    left = lane_iota((WIDTH, LANES)) < WIDTH
    for q in range(4):
        for part in range(2):
            for f in range(FIELDS):
                for j in range(4):
                    value = work[q, part, pl.ds(j * 4 + f, 16, stride=16), :]
                    high, low = split(value)
                    row = part * WIDTH + j * 16
                    s_ref[q, row : row + 16, f * LANES : (f + 1) * LANES] = high
                    s_ref[q, LANES + row : LANES + row + 16, f * LANES : (f + 1) * LANES] = low

    for q in range(4):
        products[q] = lax.dot_general(
            s_ref[q], s_ref[q, :LANES], (((1,), (1,)), ((), ())), preferred_element_type=F32
        )

    tiles = [None] * 8
    for q in range(4):
        cross = products[q, LANES:]
        full = products[q, :LANES] + (cross + cross.T)
        low = pltpu.roll(full[WIDTH:], WIDTH, 1)
        tile = full[:WIDTH] + jnp.where(left, low, -low)
        for p in range(2):
            tiles[p * 4 + q] = jnp.concatenate(
                [tile[p * 16 : p * 16 + 16], tile[32 + p * 16 : 48 + p * 16]], axis=0
            )
    for a, tile in enumerate(block_transpose(tiles)):
        mixed[a * 32 : (a + 1) * 32, :] = tile
    lane, sub, parity, _, column = places()
    for m in range(16):
        near = mixed[pl.ds(m % 2 * 16 + m // 2, 8, stride=32), :]
        far_m = 31 - m
        far = mixed[pl.ds(far_m % 2 * 16 + far_m // 2, 8, stride=32), :]
        far = reverse_rows(far, lane, sub)
        line = 2 * m + parity
        far = jnp.where(column == line, pltpu.roll(far, 4, 0), far)
        upper = (column > line) | ((column == line) & (sub < 4))
        out_ref[m * 8 : (m + 1) * 8, :] = jnp.where(upper, near, far)


def twiddles(weight, shifts):
    t = lax.axis_index("tm")
    root = jnp.sqrt(jnp.concatenate([weight[...]] * 4, axis=0))
    out = []
    for d in shifts:
        re, im = source_twiddle(t, d)
        out.append((root * re, root * im))
    return out


def twisted(source, s, rows, tw):
    re = source[0, s, rows, :].astype(F32)
    im = source[1, s, rows, :].astype(F32)
    return re * tw[0] - im * tw[1], re * tw[1] + im * tw[0]


def even_kernel(own, near2, weight, even_ref):
    tw = twiddles(weight, (0, 2))

    def step(index, _):
        rows = pl.ds(pl.multiple_of(index * 16, 16), 16)
        for s in range(2):
            y0 = twisted(own, s, rows, tw[0])
            y2 = twisted(near2, s, rows, tw[1])
            even_ref[s, 0, rows, :] = y0[0] + y2[0]
            even_ref[s, 1, rows, :] = y0[1] + y2[1]
            even_ref[s, 2, rows, :] = y0[0] - y2[0]
            even_ref[s, 3, rows, :] = y0[1] - y2[1]
        return 0

    lax.fori_loop(0, ROWS // 16, step, 0)


def send_kernel(near3, near1, weight, even, other_ref, s_ref, send_ref, work, mixed, products):
    t = lax.axis_index("tm")
    side = jnp.where(lax.axis_index("space") % 2 == 0, -1.0, 1.0).astype(F32)
    tw = twiddles(weight, (1, 3))
    tq = []
    for q in range(4):
        re, im = second_twiddle(t, q)
        tq.append((re * side, im * side))

    def step(index, _):
        rows = pl.ds(pl.multiple_of(index * 16, 16), 16)
        radix = []
        for s in range(2):
            y1 = twisted(near1, s, rows, tw[0])
            y3 = twisted(near3, s, rows, tw[1])
            a = (even[s, 0, rows, :], even[s, 1, rows, :])
            b = (even[s, 2, rows, :], even[s, 3, rows, :])
            c = (y1[0] + y3[0], y1[1] + y3[1])
            e = (y1[0] - y3[0], y1[1] - y3[1])
            radix.append(
                [
                    (a[0] + c[0], a[1] + c[1]),
                    (b[0] - e[1], b[1] + e[0]),
                    (a[0] - c[0], a[1] - c[1]),
                    (b[0] + e[1], b[1] - e[0]),
                ]
            )
        for q in range(4):
            x0 = radix[0][q]
            x1 = radix[1][q]
            v = (x1[0] * tq[q][0] - x1[1] * tq[q][1], x1[0] * tq[q][1] + x1[1] * tq[q][0])
            work[q, 0, rows, :] = x0[0] + v[0]
            work[q, 1, rows, :] = x0[1] + v[1]
            other_ref[q, 0, rows, :] = x0[0] - v[0]
            other_ref[q, 1, rows, :] = x0[1] - v[1]
        return 0

    lax.fori_loop(0, ROWS // 16, step, 0)
    pack_gram(work, s_ref, send_ref, mixed, products)


def at_sub(value, index):
    return jnp.broadcast_to(value[index : index + 1, :], value.shape)


def factor_kernel(gram, out_ref, spread):
    lane, sub, parity, group, column = places()
    first = parity == 0
    sign = jnp.where(sub < 4, 1.0, -1.0).astype(F32)
    real = sub < 4
    lane_base = lane // 16 * 16

    def turn(value):
        return pltpu.roll(value, 4, 0) * sign

    def lifted(value):
        return jnp.where(first, value, pltpu.roll(value, 7, 0))

    rows = [None] * 32
    for m in range(16):
        packed = gram[m * 8 : (m + 1) * 8, :]
        rows[m] = packed
        far = reverse_rows(packed, lane, sub)
        line = 2 * (31 - m) + parity
        rows[31 - m] = jnp.where(column == line, pltpu.roll(far, 4, 0), far)

    def block_of(v, p, g):
        return gather_lanes(v, lane % WIDTH // 16 * 16 + p * WIDTH + g)

    block = [block_of(rows[r // 2], r % 2, 0) for r in range(4)]
    for g in range(16):
        last = g == 15
        full, ahead, following = [], [], []
        for v in (rows[2 * g], rows[2 * g + 1]):
            turned = pltpu.roll(v, WIDTH, 1)
            full += [jnp.where(first, v, turned), jnp.where(first, turned, v)]
        if not last:
            ahead = [block_of(rows[2 * g + r // 2], r % 2, g + 1) for r in range(4)]
            following = [block_of(rows[2 * g + 2 + r // 2], r % 2, g + 1) for r in range(4)]
        in_group = group == g
        root, scaled = [], []
        for s in range(4):
            here = in_group & (sub % 4 == s)
            pivot = at_sub(block[s], s)
            ip = 1.0 / pivot
            root.append(lax.rsqrt(pivot))
            full[s] = jnp.where(here, jnp.where(real, 1.0, 0.0), full[s])
            y = full[s] * ip
            y_t = turn(y)
            b = block[s] * ip
            b_t = turn(b)
            if not last:
                n = ahead[s] * ip
                n_t = turn(n)
                for r in range(4):
                    mr = at_sub(ahead[s], r)
                    mi = at_sub(ahead[s], 4 + r)
                    following[r] = following[r] - (mr * n + mi * n_t)
            for r in range(s + 1, 4):
                mr = at_sub(block[s], r)
                mi = at_sub(block[s], 4 + r)
                full[r] = jnp.where(here, 0.0, full[r]) - (mr * y + mi * y_t)
                block[r] = block[r] - (mr * b + mi * b_t)
                if not last:
                    ahead[r] = ahead[r] - (mr * n + mi * n_t)
            later = in_group & (sub % 4 > s)
            scaled.append((jnp.where(later, 0.0, y), jnp.where(later, 0.0, y_t)))
        raised = [lifted(full[r]) for r in range(4)]
        for h in range(g + 1, 16):
            if h == g + 1:
                multi = [lifted(ahead[r]) for r in range(4)]
            else:
                multi = [gather_lanes(raised[r], lane_base + h) for r in range(4)]
            for odd in range(2):
                m = 2 * h + odd
                value = jnp.where(in_group, 0.0, rows[m])
                terms = []
                for r in range(4):
                    y, y_t = scaled[r]
                    terms.append(at_sub(multi[r], 2 * odd) * y + at_sub(multi[r], 4 + 2 * odd) * y_t)
                rows[m] = value - ((terms[0] + terms[1]) + (terms[2] + terms[3]))
        block = following
        for odd in range(2):
            m = 2 * g + odd
            spread[m * 8 : (m + 1) * 8, :] = jnp.where(
                first, full[2 * odd] * root[2 * odd], full[2 * odd + 1] * root[2 * odd + 1]
            )
        if g % 4 == 3:
            k = g // 4
            tiles = [spread[pl.ds(k * WIDTH + a, 8, stride=8), :] for a in range(8)]
            for b, tile in enumerate(block_transpose(tiles)):
                row = b // 4 * 32 + k * 8
                out_ref[b % 4, row : row + 8, :] = tile


def modes_kernel(slot, *refs):
    if slot == 0:
        source, s_ref, weight = refs[:3]
    else:
        source, s_ref, weight, _, _ = refs[:5]
    modes_ref, upper_ref, work, natural, modes_own, upper_own, modes_sem, upper_sem = refs[-8:]
    t = lax.axis_index("tm")
    mine = (lax.axis_index("space") + slot) % 2
    wide = (WIDTH, LANES)
    lane = lane_iota(wide)
    order = lax.broadcasted_iota(jnp.int32, wide, 0)
    line = order % 32 * 2 + order // 32
    column = lane % 16 * 4 + lane // 16 % 4
    left = lane < WIDTH
    lane8 = lane_iota(SMALL)
    natural_index = lane8 // WIDTH * WIDTH + lane8 % 4 * 16 + lane8 % WIDTH // 4
    root = lax.rsqrt(weight[...])

    copies = []
    for k in range(4):
        q = mine * 4 + k
        both = source[k]
        inverse = jnp.where(column <= line, both, 0.0)
        diag = jnp.where(left, 1.0 / both, 0.0)
        upper = jnp.where(column > line, both, jnp.where(column == line, diag, 0.0))
        for j in range(8):
            piece = gather_lanes(upper[j * 8 : j * 8 + 8], natural_index)
            natural[k, pl.ds(j // 4 + j % 4 * 16, 8, stride=2), :] = piece
        upper_own[0, k] = natural[k, :, :WIDTH]
        upper_own[1, k] = natural[k, :, WIDTH:]
        copies.append(
            pltpu.make_async_copy(upper_own.at[:, k], upper_ref.at[:, q], upper_sem.at[k])
        )
        copies[-1].start()
        swapped = pltpu.roll(inverse, WIDTH, 1)
        swapped = jnp.where(left, -swapped, swapped)
        pr = by_bin(t, [(1, 0, -1, 0)[b * k % 4] for b in range(4)])
        pi = by_bin(t, [(0, -1, 0, 1)[b * k % 4] for b in range(4)])
        lhs = jnp.concatenate([pr * inverse - pi * swapped, pr * swapped + pi * inverse], axis=0)
        lh, ll = split(lhs)
        out = jnp.dot(jnp.concatenate([lh, lh], axis=1), s_ref[k], preferred_element_type=F32)
        out = out + jnp.dot(ll, s_ref[k, :LANES], preferred_element_type=F32)
        for part in range(2):
            for f in range(FIELDS):
                for p in range(2):
                    row = part * WIDTH + p * 32
                    block = out[row : row + 32, f * LANES : (f + 1) * LANES] * root[f : f + 1, :]
                    work[k % 2, pl.ds(part * ROWS + p * 4 + f, 32, stride=8), :] = block
            modes_own[part, k] = work[k % 2, part * ROWS : (part + 1) * ROWS, :].astype(BF16)
        copies.append(
            pltpu.make_async_copy(modes_own.at[:, k], modes_ref.at[:, q], modes_sem.at[k])
        )
        copies[-1].start()
    for copy in copies:
        copy.wait()


def vmem():
    return pl.BlockSpec(memory_space=pltpu.VMEM)


HALF = (LANES, LANES)
PARAMS = pltpu.CompilerParams(vmem_limit_bytes=32 * 1024 * 1024)


def run_even(own, near2, weights):
    return pl.pallas_call(
        even_kernel,
        name="even",
        out_shape=jax.ShapeDtypeStruct((2, 4, ROWS, LANES), F32),
        in_specs=[vmem()] * 3,
        out_specs=vmem(),
        compiler_params=PARAMS,
        cost_estimate=pl.CostEstimate(flops=2**22, bytes_accessed=2**21, transcendentals=0),
    )(own, near2, weights)


def run_send(near3, near1, weights, even):
    return pl.pallas_call(
        send_kernel,
        name="send_gram",
        out_shape=(
            jax.ShapeDtypeStruct((4, 2, ROWS, LANES), F32),
            jax.ShapeDtypeStruct((4, 2 * LANES, FIELDS * LANES), BF16),
            jax.ShapeDtypeStruct(HALF, F32),
        ),
        in_specs=[vmem()] * 4,
        out_specs=(vmem(),) * 3,
        scratch_shapes=[
            pltpu.VMEM((4, 2, ROWS, LANES), F32),
            pltpu.VMEM((ROWS, LANES), F32),
            pltpu.VMEM((4, 2 * LANES, LANES), F32),
        ],
        compiler_params=PARAMS,
    )(near3, near1, weights, even)


def run_keep(work):
    return pl.pallas_call(
        pack_gram,
        name="keep_gram",
        out_shape=(
            jax.ShapeDtypeStruct((4, 2 * LANES, FIELDS * LANES), BF16),
            jax.ShapeDtypeStruct(HALF, F32),
        ),
        in_specs=[vmem()],
        out_specs=(vmem(),) * 2,
        scratch_shapes=[
            pltpu.VMEM((ROWS, LANES), F32),
            pltpu.VMEM((4, 2 * LANES, LANES), F32),
        ],
        compiler_params=PARAMS,
        cost_estimate=pl.CostEstimate(flops=3 * 10**8, bytes_accessed=2**21, transcendentals=0),
    )(work)


def run_factor(gram):
    return pl.pallas_call(
        factor_kernel,
        name="factor",
        out_shape=jax.ShapeDtypeStruct((4, WIDTH, LANES), F32),
        in_specs=[vmem()],
        out_specs=vmem(),
        scratch_shapes=[pltpu.VMEM((2 * LANES, LANES), F32)],
        compiler_params=PARAMS,
    )(gram)


def run_modes(slot, factor, s, weights, outputs=()):
    anywhere = pl.BlockSpec(memory_space=pl.ANY)
    return pl.pallas_call(
        functools.partial(modes_kernel, slot),
        name="modes_far" if slot else "modes_own",
        out_shape=(
            jax.ShapeDtypeStruct((2, SUBS, ROWS, LANES), BF16),
            jax.ShapeDtypeStruct((2, SUBS, WIDTH, WIDTH), F32),
        ),
        in_specs=[vmem()] * 3 + [anywhere] * len(outputs),
        out_specs=(anywhere, anywhere),
        scratch_shapes=[
            pltpu.VMEM((2, 2 * ROWS, LANES), F32),
            pltpu.VMEM((4, WIDTH, LANES), F32),
            pltpu.VMEM((2, 4, ROWS, LANES), BF16),
            pltpu.VMEM((2, 4, WIDTH, WIDTH), F32),
            pltpu.SemaphoreType.DMA((4,)),
            pltpu.SemaphoreType.DMA((4,)),
        ],
        input_output_aliases={3: 0, 4: 1} if outputs else {},
        compiler_params=PARAMS,
        cost_estimate=pl.CostEstimate(flops=3 * 10**8, bytes_accessed=2**22, transcendentals=0),
    )(factor, s, weights, *outputs)


def space_perm(first, shift):
    pairs = []
    for i in range(32):
        z, x, core = i // 8, i // 2 % 4, i % 2
        if shift == 0:
            core = 1 - core
        elif first == (core == 0):
            x = (x + shift) % 4
        else:
            z = (z + shift) % 4
        pairs.append((i, (z * 4 + x) * 2 + core))
    return pairs


def sum_over_chips(value):
    for first in (True, False):
        far = [lax.ppermute(value, "space", space_perm(first, d)) for d in (3, 1, 2)]
        value = ((value + far[0]) + far[1]) + far[2]
    return value


def on_device(spectra, weights):
    t = lax.axis_index("tm")
    flat = spectra.reshape(2, 2, 4, ROWS, LANES)

    def piece(d, source):
        return lax.dynamic_index_in_dim(source, (t + d) % 4, 2, keepdims=False)

    def move(d, source):
        return lax.ppermute(piece(d, source), "tm", [(i, (i + d) % 4) for i in range(4)])

    near = {}
    first = piece(2, flat)
    later, first = lax.optimization_barrier((flat, first))
    near[2] = lax.ppermute(first, "tm", [(i, (i + 2) % 4) for i in range(4)])
    for d in (3, 1):
        near[d] = move(d, later)
    last, near[2] = lax.optimization_barrier((flat, near[2]))
    own = piece(0, last)
    even = run_even(own, near[2], weights)
    other, s_far, send = run_send(near[3], near[1], weights, even)
    across = space_perm(True, 0)
    arrived = lax.ppermute(send, "space", across)
    s_own, keep = run_keep(other)
    gram = sum_over_chips(keep + arrived)
    factor = run_factor(gram)
    far = lax.ppermute(factor, "space", across)
    outputs = run_modes(0, factor, s_own, weights)
    modes, upper = run_modes(1, far, s_far, weights, outputs)
    return (
        modes.reshape(2, SUBS, 1, WIDTH, FIELDS, LANES),
        upper.reshape(2, SUBS, 1, WIDTH, WIDTH),
    )


def solution(mesh):
    placed = (P(None, "tm", None, None, None, "space"), P(None, "space"))
    return jax.shard_map(
        on_device,
        mesh=mesh,
        in_specs=placed,
        out_specs=(P(None, None, "tm", None, None, "space"), P(None, None, "tm", None, None)),
        check_vma=False,
    )
```
